32 devices in a mesh: section: 2 (over core), fsdp: 2 (over x), tok: 8 (over z, y).
Axes of the slice: x: 2, y: 2, z: 4, core: 2. Of those that a mesh axis runs over, the one named last changes fastest.
Arguments:
- hidden: bfloat16 [4, 32, 3072], P(None, 'tok'), may hold values from -6 to 6
- lengths: int32 [4], replicated, may hold values from 1 to 32, 96 in all
- text_count: int32 [1], replicated, may hold values from 1 to 32
- timestep: int32 [1], replicated, may hold values from 0 to 49
- mod_table: bfloat16 [2, 50, 6, 3072], P('section'), may hold values from -3 to 3
- w_qkv: bfloat16 [2, 3072, 3, 1536], P('section', 'tok', None, 'fsdp'), may hold values from -0.109375 to 0.109375
- w_out: bfloat16 [2, 3072, 1536], P('section', 'tok', 'fsdp'), may hold values from -0.15625 to 0.15625
- qk_gain: float32 [2, 2, 64], P('section'), may hold values from 0.5 to 2
- stale_cache: bfloat16 [2, 2, 4, 32, 1536], P('section', None, None, None, 'fsdp'), may hold values from -6 to 6
Outputs:
- layer_out: bfloat16 [2, 4, 32, 3072], P('section', None, 'tok')
- new_cache: bfloat16 [2, 2, 4, 32, 1536], P('section', None, None, None, 'fsdp')
The draws below stay inside these ranges and needn't reach their ends.
Inputs may be any that keep to these rules, and one draw needn't show every extreme that they name: The lengths sum to 96; one patch is full with exactly 32 live tokens.
All inputs are finite; a program needn't handle non-finite values.
Results may differ from the reference program's by a relative error of at most 0.012.
Values may be sent and summed in bfloat16 or wider, within the bound.
No kernel may reach another device: no remote copies, remote signals or barrier semaphores. Data moves between devices by JAX's collectives and lax.ppermute only.
A program may use at most 128 MiB of HBM per device.

```python
import math
import jax
import jax.numpy as jnp
import numpy as np
from jax import lax

D = 3072
HEADS = 24
HEAD_DIM = 64
PATCHES = 4
STEPS = 50
HD = 1536
CAP = 32
LIVE = 96
SECTIONS = 2


def block_scale(key, dims, cuts, smallest, largest):
    gain, own = 1.0, jax.random.fold_in(key, 6)
    for axis_at, parts in cuts:
        heights = jnp.exp(jax.random.uniform(jax.random.fold_in(own, axis_at), (parts,), jnp.float32, smallest / len(cuts), largest / len(cuts)))
        gain = gain * jnp.repeat(heights, dims[axis_at] // parts).reshape([-1 if axis == axis_at else 1 for axis in range(len(dims))])
    return gain


def split_up(number_of, total, limit, skew):
    loads = [(1 << 20) // math.isqrt(rank ** skew) + 1 for rank in range(2, number_of + 1)]
    rest, counts = total - limit - (number_of - 1), [1] * (number_of - 1)
    while rest > 0:
        free = [i for i in range(number_of - 1) if counts[i] < limit]
        whole, remaining = sum([loads[i] for i in free]), rest
        for i in free:
            more = min(limit - counts[i], max(1, remaining * loads[i] // whole), rest)
            counts[i] = counts[i] + more
            rest = rest - more
    return np.array([limit] + counts)


def uneven_parts(key, number_of, total, limit, skew):
    if number_of == 2:
        one = jax.random.randint(key, (), max(1, total - limit), min(limit, total - 1) + 1)
        return jnp.stack([one, total - one])
    tallies = jnp.asarray(split_up(number_of, total, limit, skew), jnp.int32)
    pairs = (number_of - 1) // 2
    source_of, sink = tallies[1:1 + 2 * pairs:2], tallies[2:2 + 2 * pairs:2]
    slack = jnp.minimum(source_of - 1, limit - sink)
    moved = jax.random.randint(jax.random.fold_in(key, 1), (pairs,), 0, 1 << 20) % (slack + 1)
    tallies = tallies.at[1:1 + 2 * pairs:2].set(source_of - moved).at[2:2 + 2 * pairs:2].set(sink + moved)
    return tallies[jax.random.permutation(jax.random.fold_in(key, 2), number_of)]


def gaussian(rng, shape, scale, reach, cuts=(), kind=jnp.bfloat16):
    drawn = scale * jax.random.normal(rng, shape, jnp.float32)
    if cuts:
        drawn = drawn * block_scale(rng, shape, cuts, -0.22, 0.18)
    return jnp.clip(drawn, -reach, reach).astype(kind)


def setup_inputs(seed: int = 0) -> dict:
    splits = jax.random.split(jax.random.key(seed), 10)
    return {
        "hidden": gaussian(splits[0], (PATCHES, CAP, D), 1.0, 6.0, ((1, 8),)),
        "lengths": uneven_parts(splits[1], PATCHES, LIVE, CAP, 0).astype(jnp.int32),
        "text_count": jax.random.randint(splits[2], (1,), 1, CAP + 1).astype(jnp.int32),
        "timestep": jax.random.randint(splits[3], (1,), 0, STEPS).astype(jnp.int32),
        "mod_table": gaussian(splits[4], (SECTIONS, STEPS, 6, D), 0.5, 3.0, ((0, 2),)),
        "w_qkv": gaussian(splits[5], (SECTIONS, D, 3, HD), D ** -0.5, 0.109375, ((0, 2), (1, 8), (3, 2))),
        "w_out": gaussian(splits[6], (SECTIONS, D, HD), HD ** -0.5, 0.15625, ((0, 2), (1, 8), (2, 2))),
        "qk_gain": jnp.clip(jnp.exp(math.log(2.0) - 1.3862944 * jax.random.uniform(splits[7], (SECTIONS, 2, HEAD_DIM), jnp.float32) ** block_scale(splits[7], (SECTIONS, 2, HEAD_DIM), ((0, 2),), -0.2, 0.2)), 0.5, 2.0),
        "stale_cache": gaussian(splits[8], (SECTIONS, 2, PATCHES, CAP, HD), 1.0, 6.0, ((0, 2), (4, 2))),
    }


def layer_norm(values, eps):
    mean = lax.optimization_barrier(jnp.mean(values, axis=-1, keepdims=True))
    centred = values - mean
    spread = lax.optimization_barrier(jnp.mean(centred * centred, axis=-1, keepdims=True))
    return centred * lax.rsqrt(spread + eps)

def modulate(inputs, positions, modulation, text_total):
    is_text = (positions < text_total)[:, None]
    shift = jnp.where(is_text, modulation[3], modulation[0])
    scale = jnp.where(is_text, modulation[4], modulation[1])
    gate = jnp.where(is_text, modulation[5], modulation[2])
    normed = layer_norm(inputs, 1e-05)
    return ((normed * (1.0 + scale) + shift).astype(jnp.bfloat16), gate)

def project_heads(mixed, gains):
    queries = (layer_norm(mixed[:, 0], 1e-06) * gains[0]).astype(jnp.bfloat16)
    keys_new = (layer_norm(mixed[:, 1], 1e-06) * gains[1]).astype(jnp.bfloat16)
    values_new = mixed[:, 2].astype(jnp.bfloat16)
    return (queries, keys_new, values_new)

def attend(queries, keys_all, values_all, key_live):
    scores = jnp.einsum('qhd,khd->hqk', queries.astype(jnp.float32), keys_all.astype(jnp.float32)) * HEAD_DIM ** (-0.5)
    scores = jnp.where(key_live[None, None, :], scores, -jnp.inf)
    top = lax.optimization_barrier(jnp.max(scores, axis=-1, keepdims=True))
    expo = jnp.exp(scores - top)
    weights = (expo / lax.optimization_barrier(jnp.sum(expo, axis=-1, keepdims=True))).astype(jnp.bfloat16)
    return jnp.einsum('hqk,khd->qhd', weights.astype(jnp.float32), values_all.astype(jnp.float32)).astype(jnp.bfloat16)

def reference(hidden, lengths, text_count, timestep, mod_table, w_qkv, w_out, qk_gain, stale_cache):
    offsets = jnp.cumsum(lengths) - lengths
    slots = jnp.arange(CAP, dtype=jnp.int32)
    key_live = (slots[None, :] < lengths[:, None]).reshape(-1)
    section_in = hidden
    outputs = []
    caches = []
    for section in range(SECTIONS):
        modulation = lax.dynamic_index_in_dim(mod_table[section], timestep[0], 0, keepdims=False).astype(jnp.float32)
        weight_in = w_qkv[section].reshape(D, 3 * HD)
        cache_keys = stale_cache[section, 0].reshape(PATCHES, CAP, HEADS, HEAD_DIM)
        cache_values = stale_cache[section, 1].reshape(PATCHES, CAP, HEADS, HEAD_DIM)
        results = []
        for patch in range(PATCHES):
            inputs = section_in[patch].astype(jnp.float32)
            row_live = slots < lengths[patch]
            modded, gate = modulate(inputs, offsets[patch] + slots, modulation, text_count[0])
            mixed = jnp.dot(modded, weight_in, preferred_element_type=jnp.float32).reshape(CAP, 3, HEADS, HEAD_DIM)
            queries, keys_new, values_new = project_heads(mixed, qk_gain[section])
            keys_new = jnp.where(row_live[:, None, None], keys_new, jnp.zeros_like(keys_new))
            values_new = jnp.where(row_live[:, None, None], values_new, jnp.zeros_like(values_new))
            cache_keys = cache_keys.at[patch].set(keys_new)
            cache_values = cache_values.at[patch].set(values_new)
            attended = attend(queries, cache_keys.reshape(-1, HEADS, HEAD_DIM), cache_values.reshape(-1, HEADS, HEAD_DIM), key_live).reshape(CAP, HD)
            projected = lax.dot_general(attended, w_out[section], (((1,), (1,)), ((), ())), preferred_element_type=jnp.float32)
            result = jnp.where(row_live[:, None], inputs + gate * projected, 0.0).astype(jnp.bfloat16)
            results.append(result)
        section_in = jnp.stack(results)
        outputs.append(section_in)
        caches.append(jnp.stack([cache_keys.reshape(PATCHES, CAP, HD), cache_values.reshape(PATCHES, CAP, HD)]))
    return (jnp.stack(outputs), jnp.stack(caches))
```

```python
import collections
import functools
import math

import jax
import jax.numpy as jnp
from jax import lax
from jax.experimental import pallas as pl
from jax.experimental.pallas import tpu as pltpu
from jax.sharding import PartitionSpec as P

HEAD_DIM = 64
F32 = jnp.float32
BF16 = jnp.bfloat16
MOST_PEERS = 8


def swap(block, axis):
    size = lax.axis_size(axis)
    return lax.ppermute(block, axis, [(i, size - 1 - i) for i in range(size)])


def exchange(blocks):
    return lax.all_to_all(blocks, "tok", 0, 0, tiled=False)


def gather(block):
    count = lax.axis_size("tok")
    return exchange(jnp.broadcast_to(block[None], (count,) + block.shape))


def layer_norm(values, eps):
    mean = jnp.mean(values, axis=-1, keepdims=True)
    centred = values - mean
    spread = jnp.mean(centred * centred, axis=-1, keepdims=True)
    return centred * lax.rsqrt(spread + eps)


def three_terms(values):
    high = lax.reduce_precision(values, 8, 7)
    rest = values - high
    middle = lax.reduce_precision(rest, 8, 7)
    return jnp.concatenate([high, middle, rest - middle], axis=-1).astype(BF16)


def from_three(terms):
    terms = terms.astype(F32)
    count = terms.shape[-1] // 3
    return terms[..., :count] + terms[..., count : 2 * count] + terms[..., 2 * count :]


def by_all_to_all(hidden, lengths, text_count, timestep, mod_table, w_qkv, w_out, qk_gain, stale_cache):
    first = lax.axis_index("section") == 0
    own_half = lax.axis_index("section")
    tok_count = lax.axis_size("tok")
    tok_index = lax.axis_index("tok")
    patches, cap_dev, width = hidden.shape
    rows = patches * cap_dev
    total = rows * tok_count
    depth = w_qkv.shape[1]
    half = w_qkv.shape[3] // 2
    heads = half // HEAD_DIM

    def both_layers(own, other):
        return jnp.where(first, own, other), jnp.where(first, other, own)

    def halves(array):
        axis = array.ndim - 1
        keep = lax.dynamic_slice_in_dim(array, own_half * half, half, axis)
        send = lax.dynamic_slice_in_dim(array, (1 - own_half) * half, half, axis)
        return both_layers(keep, swap(send, "section"))

    offsets = jnp.cumsum(lengths) - lengths
    row = jnp.arange(total, dtype=jnp.int32)
    row_patch = (row // cap_dev) % patches
    row_slot = (row // rows) * cap_dev + row % cap_dev
    row_live = row_slot < lengths[row_patch]
    is_text = ((offsets[row_patch] + row_slot) < text_count[0])[:, None]
    own_patch = jnp.arange(rows, dtype=jnp.int32) // cap_dev
    own_live = (tok_index * cap_dev + jnp.arange(rows, dtype=jnp.int32) % cap_dev) < lengths[own_patch]
    cap_all = cap_dev * tok_count
    stale_patch = jnp.arange(patches * cap_all, dtype=jnp.int32) // cap_all
    stale_live = (jnp.arange(patches * cap_all, dtype=jnp.int32) % cap_all) < lengths[stale_patch]
    fresh_seen = row_live[None, :] & (row_patch[None, :] <= own_patch[:, None])
    stale_seen = stale_live[None, :] & (stale_patch[None, :] > own_patch[:, None])
    seen = jnp.concatenate([fresh_seen, stale_seen], axis=1)

    states = hidden.reshape(rows, width).astype(F32)
    mean = jnp.mean(states, axis=-1, keepdims=True)
    centred = states - mean
    inverse = lax.rsqrt(jnp.mean(centred * centred, axis=-1, keepdims=True) + 1e-05)
    stats = three_terms(jnp.concatenate([mean, inverse], axis=-1))
    stats = jnp.pad(stats, ((0, 0), (0, 128 - stats.shape[1])))
    blocks = hidden.reshape(rows, tok_count, depth).transpose(1, 0, 2)
    blocks = jnp.concatenate(
        [blocks, jnp.broadcast_to(stats[None], (tok_count,) + stats.shape)], axis=-1
    )
    arrived = exchange(blocks).reshape(total, depth + 128)
    slices = arrived[:, :depth].astype(F32)
    stats = from_three(arrived[:, depth : depth + 6])

    weight_in = halves(w_qkv[0].transpose(1, 0, 2))
    weight_out = halves(w_out[0])
    stale = halves(stale_cache[0].reshape(2, patches * cap_all, 2 * half))
    modulation = lax.dynamic_index_in_dim(mod_table[0], timestep[0], 0, keepdims=False)
    modulation = lax.dynamic_slice_in_dim(modulation, tok_index * depth, depth, 1)
    modulation = both_layers(modulation, swap(modulation, "section"))
    gains = both_layers(qk_gain[0], swap(qk_gain[0], "section"))

    outputs, caches = [], []
    for layer in range(2):
        if layer:
            part_mean = jnp.mean(slices, axis=-1, keepdims=True)
            off = slices - part_mean
            part = jnp.concatenate([part_mean, jnp.sum(off * off, axis=-1, keepdims=True)], axis=-1)
            parts = gather(part)
            mean = jnp.mean(parts[..., 0], axis=0)
            apart = parts[..., 0] - mean[None]
            spread = jnp.sum(parts[..., 1] + depth * apart * apart, axis=0) / (depth * tok_count)
            stats = jnp.stack([mean, lax.rsqrt(spread + 1e-05)], axis=-1)
        mod = modulation[layer].astype(F32)
        shift = jnp.where(is_text, mod[3], mod[0])
        scale = jnp.where(is_text, mod[4], mod[1])
        gate = jnp.where(is_text, mod[5], mod[2])
        normed = (slices - stats[:, :1]) * stats[:, 1:]
        modded = (normed * (1.0 + scale) + shift).astype(BF16)
        partial = jnp.concatenate(
            [
                jnp.dot(modded, weight_in[layer][i], preferred_element_type=F32).astype(BF16)
                for i in range(3)
            ],
            axis=-1,
        ).reshape(tok_count, rows, 3 * half)
        mixed = jnp.sum(exchange(partial).astype(F32), axis=0).reshape(rows, 3, heads, HEAD_DIM)
        gain = gains[layer]
        queries = (layer_norm(mixed[:, 0], 1e-06) * gain[0]).astype(BF16)
        keys_new = (layer_norm(mixed[:, 1], 1e-06) * gain[1]).astype(BF16)
        fresh = jnp.stack([keys_new, mixed[:, 2].astype(BF16)])
        fresh = jnp.where(own_live[None, :, None, None], fresh, jnp.zeros_like(fresh))
        fresh = gather(fresh.reshape(2, rows, half))
        caches.append(fresh)
        fresh = fresh.transpose(1, 0, 2, 3).reshape(2, total, half)
        keys_values = jnp.concatenate([fresh, stale[layer]], axis=1).reshape(
            2, total + patches * cap_all, heads, HEAD_DIM
        )
        scores = (
            jnp.einsum("qhd,khd->hqk", queries, keys_values[0], preferred_element_type=F32)
            * HEAD_DIM ** (-0.5)
        )
        scores = jnp.where(seen[None], scores, -jnp.inf)
        expo = jnp.exp(scores - jnp.max(scores, axis=-1, keepdims=True))
        weights = (expo / jnp.sum(expo, axis=-1, keepdims=True)).astype(BF16)
        attended = jnp.einsum("hqk,khd->qhd", weights, keys_values[1], preferred_element_type=F32)
        attended = gather(attended.astype(BF16).reshape(rows, half)).reshape(total, half)
        projected = lax.dot_general(
            attended, weight_out[layer], (((1,), (1,)), ((), ())), preferred_element_type=F32
        ).astype(BF16)
        projected = projected.astype(F32) + swap(projected, "section").astype(F32)
        projected = projected.astype(BF16)
        projected = projected.astype(F32) + swap(projected, "fsdp").astype(F32)
        result = jnp.where(row_live[:, None], slices + gate * projected, 0.0).astype(BF16)
        outputs.append(result)
        slices = result.astype(F32)

    final = jnp.where(first, outputs[0], outputs[1]).reshape(tok_count, rows, depth)
    final = exchange(final).transpose(1, 0, 2).reshape(1, patches, cap_dev, width)
    mine = jnp.where(first, caches[0], caches[1])
    theirs = swap(jnp.where(first, caches[1], caches[0]), "section")
    cache = jnp.concatenate(
        [jnp.where(first, mine, theirs), jnp.where(first, theirs, mine)], axis=-1
    ).reshape(tok_count, 2, patches, cap_dev, 2 * half)
    cache = cache.transpose(1, 2, 0, 3, 4).reshape(1, 2, patches, cap_all, 2 * half)
    return final, cache


def iota(shape, dim):
    return lax.broadcasted_iota(jnp.int32, shape, dim)


def total_of(parts):
    total = parts[0]
    for part in parts[1:]:
        total = total + part
    return total


def split_three(value):
    high = value.astype(BF16).astype(F32)
    middle = (value - high).astype(BF16).astype(F32)
    return [high, middle, value - high - middle]


def in_lanes(columns, lanes):
    rows = columns[0].shape[0]
    lane = iota((rows, lanes), 1)
    block = jnp.zeros((rows, lanes), F32)
    for i, column in enumerate(columns):
        block = jnp.where(lane == i, column, block)
    return block.astype(BF16)


def from_columns(block, at):
    return [
        sum(block[:, at + i : at + i + 1] for i in range(3 * j, 3 * j + 3)) for j in range(2)
    ]


def bounds(sizes, patches):
    ends = [sizes[0]]
    for p in range(1, patches):
        ends.append(ends[-1] + sizes[p])
    return ends


def positions(sizes, patch, slot, patches):
    ends = bounds(sizes, patches)
    position = jnp.full(slot.shape, -1, jnp.int32)
    for p in range(patches):
        own = (patch == p) & (slot < sizes[p])
        position = jnp.where(own, slot + (ends[p] - sizes[p]), position)
    return position


def slots_by_device(shape, dim, cap_dev, patches):
    index = iota(shape, dim)
    rows = cap_dev * patches
    return (index // cap_dev) % patches, (index // rows) * cap_dev + index % cap_dev


def slots_by_patch(shape, dim, cap_all):
    index = iota(shape, dim)
    return index // cap_all, index % cap_all


def begin(source, target, sem):
    copy = pltpu.make_async_copy(source, target, sem)
    copy.start()
    return copy


def finish(copies):
    for copy in copies:
        copy.wait()


def send_rows(dims, hidden, out, staged, sems):
    rows = dims.patches * dims.cap_dev
    given = hidden[...].astype(F32).reshape(rows, hidden.shape[2])
    mean = jnp.mean(given, axis=-1, keepdims=True)
    centred = given - mean
    inverse = lax.rsqrt(jnp.mean(centred * centred, axis=-1, keepdims=True) + 1e-05)
    stats = in_lanes(split_three(mean) + split_three(inverse), 128)
    given = given.astype(BF16)
    copies = []
    for i in range(dims.count):
        staged[i, :, : dims.depth] = given[:, i * dims.depth : (i + 1) * dims.depth]
        staged[i, :, dims.depth :] = stats
        copies.append(begin(staged.at[i], out.at[i], sems.at[i]))
    finish(copies)


def modulation_rows(dims, mod, sizes):
    is_text = iota((dims.live, 1), 0) < sizes[dims.patches]
    mod = mod[...].astype(F32)
    return [
        jnp.where(is_text, mod[i + 3 : i + 4, :], mod[i : i + 1, :]) for i in range(3)
    ]


def put_partials(dims, out, staged, sems, query, key, value, extra, stats):
    live, width, groups, turns = dims.live, dims.group_width, dims.groups, dims.turns
    share = live // turns
    fold = share // 2
    sides = query.shape[1] // (groups * width)
    copies = []
    for g in range(sides * groups):
        cut = slice(g * width, (g + 1) * width)
        pair = jnp.concatenate([key[:live, cut], value[:live, cut]], axis=1).astype(BF16)
        if extra:
            last = query[live : live + 4, cut]
            rest = [
                jnp.concatenate([key[live : live + 4, cut], value[live : live + 4, cut]], axis=1),
                jnp.concatenate([last, jnp.zeros_like(last)], axis=1),
            ]
        else:
            rest = []
        for h in range(turns):
            part = query[h * share : (h + 1) * share, cut]
            rows = [jnp.concatenate([part[:fold], part[fold:]], axis=1)] + rest
            at = (h * groups + g % groups) * sides + g // groups
            staged[at, :live, :] = pair
            rows = jnp.concatenate(rows, axis=0)
            staged[at, live : live + rows.shape[0], :] = rows.astype(BF16)
            if extra:
                staged[at, live + fold + 8 :, :] = stats
            copies.append(begin(staged.at[at], out.at[at], sems.at[at]))
    finish(copies)


def own_then_other(dims, wide):
    second = lax.axis_index("tok") % dims.pairs == 1
    left, right = wide[:, : dims.depth], wide[:, dims.depth :]
    return jnp.where(second, right, left), jnp.where(second, left, right)


def load(dims, side, weights, out, sems):
    columns = out.shape[2]
    start = pl.multiple_of(lax.axis_index("tok") % dims.pairs * columns, 128) if side else 0
    finish(
        [
            begin(weights.at[i, :, pl.ds(start, columns)], out.at[i], sems.at[i])
            for i in range(out.shape[0])
        ]
    )


def first_partials(
    dims, sizes, mod, weights, arrived, kept_states, out, staged, sems
):
    patch, slot = slots_by_device((1, dims.total), 1, dims.cap_dev, dims.patches)
    position = positions(sizes, patch, slot, dims.patches)
    pick = (iota((dims.live, dims.total), 0) == position).astype(F32).astype(BF16)
    rows = arrived[...].reshape(dims.total, dims.depth + 128)
    states = jnp.dot(pick, rows, preferred_element_type=F32)
    mean, inverse = from_columns(states, dims.depth)
    states = states[:, : dims.depth]
    own_mod = own_then_other(dims, mod[...].astype(F32))[0]
    shift, scale, gate = modulation_rows(dims, own_mod, sizes)
    modded = ((states - mean) * inverse * (1.0 + scale) + shift).astype(BF16)
    kept_states[...] = states.astype(BF16)
    mixed = [jnp.dot(modded, weights[i], preferred_element_type=F32) for i in range(3)]
    put_partials(dims, out, staged, sems, *mixed, False, None)


def head_means(values, blocks, terms):
    total = None
    for _ in range(terms):
        term = values.astype(BF16)
        part = jnp.dot(term, blocks, preferred_element_type=F32)
        total = part if total is None else total + part
        values = values - term.astype(F32)
    return total * (1.0 / HEAD_DIM)


def head_norm(values, gain, blocks):
    centred = values - head_means(values, blocks, 3)
    spread = head_means(centred * centred, blocks, 2)
    return (centred * lax.rsqrt(spread + 1e-06) * gain).astype(BF16)


def own_share(dims, turn, value, share):
    part = value[:share]
    for h in range(1, dims.turns):
        part = jnp.where(turn == h, value[h * share : (h + 1) * share], part)
    return part


def attention(
    dims, layer, sizes, gains, stale, arrived, attended, cache, block, fresh_rows, sems
):
    count = arrived.shape[0]
    turn = lax.axis_index("tok") // dims.pairs // dims.groups
    live, width = dims.live, dims.group_width
    share = live // dims.turns
    fold = share // 2
    pairs = total_of([arrived[i, :live, :].astype(F32) for i in range(count)])
    height = fold + 8 if layer else fold
    folded = [arrived[i, live : live + height, :].astype(F32) for i in range(count)]
    extras = [part[fold:] for part in folded]
    folded = total_of(folded)
    queries = jnp.concatenate([folded[:fold, :width], folded[:fold, width:]], axis=0)
    if layer:
        is_text = iota((live, 1), 0) < sizes[dims.patches]
        eye = (iota((live, live), 0) == iota((live, live), 1)).astype(F32).astype(BF16)
        means, spreads = [], []
        stats = jnp.concatenate(
            [arrived[i, live + fold + 8 :, :live].astype(F32) for i in range(count)], axis=0
        )
        columns = lax.dot_general(
            eye, stats.astype(BF16), (((1,), (1,)), ((), ())), preferred_element_type=F32
        )
        for i in range(count):
            mean, spread = from_columns(columns, 8 * i)
            means.append(mean)
            spreads.append(spread)
        mean = total_of(means) * (1.0 / count)
        apart = [part - mean for part in means]
        spread = total_of(spreads) + dims.count // count * dims.depth * total_of([part * part for part in apart])
        inverse = lax.rsqrt(spread * (1.0 / (dims.count * dims.depth)) + 1e-05)
        pairs = pairs + total_of(
            [a * jnp.where(is_text, e[0:1], e[1:2]) for a, e in zip(apart, extras)]
        )
        total = total_of(extras)
        pairs = pairs * inverse + jnp.where(is_text, total[2:3], total[3:4])
        mine = functools.partial(own_share, dims, turn, share=share)
        text_mine = (iota((share, 1), 0) + turn * share) < sizes[dims.patches]
        queries = queries + total_of(
            [
                mine(a) * jnp.where(text_mine, e[4:5, :width], e[5:6, :width])
                for a, e in zip(apart, extras)
            ]
        )
        queries = queries * mine(inverse) + jnp.where(text_mine, total[6:7, :width], total[7:8, :width])
    ends = bounds(sizes, dims.patches)
    query_at = iota((share, 1), 0) + turn * share
    query_patch = jnp.zeros((share, 1), jnp.int32)
    for end in ends[:-1]:
        query_patch = query_patch + (query_at >= end).astype(jnp.int32)
    query_end = jnp.zeros((share, 1), jnp.int32)
    for p, end in enumerate(ends):
        query_end = jnp.where(query_patch == p, end, query_end)
    stale_patch, stale_slot = slots_by_patch((1, dims.total), 1, dims.cap_all)
    stale_live = positions(sizes, stale_patch, stale_slot, dims.patches) >= 0
    fresh_seen = iota((share, live), 1) < query_end
    stale_seen = stale_live & (stale_patch > query_patch)
    heads = width // HEAD_DIM
    contract = (((1,), (1,)), ((), ()))
    same = iota((width, width), 0) // HEAD_DIM == iota((width, width), 1) // HEAD_DIM
    blocks = same.astype(F32).astype(BF16)
    gain = [jnp.concatenate([gains[i : i + 1, :]] * heads, axis=1) for i in range(2)]
    query = head_norm(queries, gain[0], blocks).astype(F32)
    key = head_norm(pairs[:, :width], gain[1], blocks)
    value = pairs[:, width:].astype(BF16)
    lanes = iota((heads * share, width), 1) // HEAD_DIM == iota((heads * share, width), 0) // share
    stacked = jnp.where(lanes, jnp.concatenate([query] * heads, axis=0), 0.0).astype(BF16)
    fresh = lax.dot_general(stacked, key, contract, preferred_element_type=F32)
    old = lax.dot_general(stacked, stale[0], contract, preferred_element_type=F32)
    repeated = lambda seen: jnp.concatenate([seen.astype(jnp.int32)] * heads, axis=0) > 0
    fresh = jnp.where(repeated(fresh_seen), fresh * HEAD_DIM ** (-0.5), -jnp.inf)
    old = jnp.where(repeated(stale_seen), old * HEAD_DIM ** (-0.5), -jnp.inf)
    top = jnp.maximum(jnp.max(fresh, axis=-1, keepdims=True), jnp.max(old, axis=-1, keepdims=True))
    fresh, old = jnp.exp(fresh - top), jnp.exp(old - top)
    norm = jnp.sum(fresh, axis=-1, keepdims=True) + jnp.sum(old, axis=-1, keepdims=True)
    fresh, old = (fresh / norm).astype(BF16), (old / norm).astype(BF16)
    outs = jnp.dot(fresh, value, preferred_element_type=F32)
    outs = outs + jnp.dot(old, stale[1], preferred_element_type=F32)
    outs = jnp.where(lanes, outs, 0.0)
    outs = total_of([outs[h * share : (h + 1) * share] for h in range(heads)])
    block[...] = jnp.concatenate([outs[:fold], outs[fold:]], axis=1).astype(BF16)
    copies = [begin(block, attended.at[i], sems.at[i]) for i in range(attended.shape[0])]
    new = jnp.concatenate([key.astype(F32), pairs[:, width:]], axis=1).astype(BF16)
    patch, slot = slots_by_patch((dims.total, 1), 0, dims.cap_all)
    position = positions(sizes, patch, slot, dims.patches)
    spread_out = (iota((dims.total, live), 1) == position).astype(F32).astype(BF16)
    fresh_rows[...] = jnp.dot(spread_out, new, preferred_element_type=F32).astype(BF16)
    copies.append(begin(fresh_rows, cache, sems.at[attended.shape[0]]))
    finish(copies)


def output_rows(dims, sizes, mod, near, states, arrived):
    width = dims.group_width
    rows = []
    for h in range(dims.turns):
        parts = [
            arrived[(h * dims.groups + g) * dims.pairs + y].astype(F32)
            for y in range(dims.pairs)
            for g in range(dims.groups)
        ]
        rows.append(jnp.concatenate([part[:, :width] for part in parts], axis=1))
        rows.append(jnp.concatenate([part[:, width:] for part in parts], axis=1))
    heads = jnp.concatenate(rows, axis=0).astype(BF16)
    projected = lax.dot_general(
        heads, near[...], (((1,), (1,)), ((), ())), preferred_element_type=F32
    )
    gate = own_then_other(dims, modulation_rows(dims, mod, sizes)[2])[0]
    return (from_first(dims, states) + gate * projected).astype(BF16)


def from_first(dims, states):
    half = jnp.zeros((dims.live, 1), jnp.int32) + lax.axis_index("fsdp")
    return jnp.where(half == 0, states.astype(F32), 0.0)


def layer_rows(dims, sizes, mod, near, states, arrived, out):
    out[...] = output_rows(dims, sizes, mod, near, states[...], arrived)


def both(first, second):
    return (first[...].astype(F32) + second[...].astype(F32)).astype(BF16)


def next_partials(
    dims, sizes, mod, weights, swapped, corner, others, across, given, out, staged, sems
):
    states = [both(given, across), both(others, corner)]
    states = jnp.concatenate([part.astype(F32) for part in states], axis=1)
    mean = jnp.mean(states, axis=-1, keepdims=True)
    centred = states - mean
    spread = jnp.sum(centred * centred, axis=-1, keepdims=True)
    stats = in_lanes(split_three(mean) + split_three(spread), 128)
    eye = (iota((dims.live, dims.live), 0) == iota((dims.live, dims.live), 1)).astype(F32).astype(BF16)
    stats = lax.dot_general(stats, eye, (((0,), (0,)), ((), ())), preferred_element_type=F32)[:8]
    lanes = 2 * dims.group_width
    stats = jnp.concatenate([stats, jnp.zeros((8, lanes - dims.live), F32)], axis=1).astype(BF16)
    rows = jnp.concatenate(own_then_other(dims, mod[...].astype(F32)), axis=1)
    is_text = iota((dims.live, 1), 0) < sizes[dims.patches]
    scaled = centred * (1.0 + jnp.where(is_text, rows[4:5], rows[1:2]))
    extra = jnp.concatenate(
        [1.0 + rows[4:5], 1.0 + rows[1:2], rows[3:4], rows[0:1], jnp.zeros_like(rows[:4])], axis=0
    )
    left = jnp.concatenate([scaled, extra], axis=0).astype(BF16)
    mixed = [
        jnp.dot(left[:, : dims.depth], weights[i], preferred_element_type=F32)
        + jnp.dot(left[:, dims.depth :], swapped[i], preferred_element_type=F32)
        for i in range(3)
    ]
    put_partials(dims, out, staged, sems, *mixed, True, stats)


def last_rows(
    dims, sizes, mod, near, made, back, given, across, first_cache, last_cache, first_side,
    last_side, arrived, out, pair, pieces, staged, sems, fetched, sent
):
    def spread(states):
        patch, slot = slots_by_device((dims.total, 1), 0, dims.cap_dev, dims.patches)
        position = positions(sizes, patch, slot, dims.patches)
        pick = (iota((dims.total, dims.live), 1) == position).astype(F32).astype(BF16)
        blocks = jnp.dot(pick, states, preferred_element_type=F32).astype(BF16)
        staged[...] = blocks.reshape(staged.shape)
        finish(
            [
                begin(staged, out.at[pl.ds(i * dims.count, dims.count)], sems.at[i])
                for i in range(out.shape[0] // dims.count)
            ]
        )

    def fetch(cache, side):
        copy = begin(cache, pieces.at[0], fetched)
        pieces[1] = side[...]
        return copy

    section = lax.axis_index("section")

    @pl.when(section == 0)
    def _():
        fetching = fetch(first_cache, first_side)
        states = from_first(dims, both(made, back)).astype(BF16)
        fetching.wait()
        copy = begin(pieces, pair, sent)
        spread(states)
        copy.wait()

    @pl.when(section != 0)
    def _():
        fetching = fetch(last_cache, last_side)
        states = output_rows(dims, sizes, mod, near, both(given, across), arrived)
        fetching.wait()
        copy = begin(pieces, pair, sent)
        spread(states)
        copy.wait()


def join(dims, arrived, pair, other, out, cache, pieces):
    for i in range(dims.count):
        block = arrived[i].astype(F32) + arrived[dims.count + i].astype(F32)
        block = block.reshape(dims.patches, dims.cap_dev, dims.depth)
        out[0, :, :, i * dims.depth : (i + 1) * dims.depth] = block.astype(BF16)
    groups, width, pairs = dims.groups, dims.group_width, dims.pairs
    own = lax.axis_index("tok")
    line, side = own // pairs, own % pairs
    for g, blocks in enumerate((pair, other)):
        for y in range(pairs):
            pieces[(side ^ y) * groups + (line % groups ^ g)] = blocks[y]
    for i in range(2):
        cut = slice(i * width, (i + 1) * width)
        cache[i] = jnp.concatenate([pieces[j][:, cut] for j in range(groups * pairs)], axis=1)


Dims = collections.namedtuple(
    "Dims",
    [
        "count",
        "pairs",
        "patches",
        "cap_dev",
        "cap_all",
        "total",
        "live",
        "depth",
        "groups",
        "turns",
        "group_width",
    ],
)


class Stays:
    def __init__(self, *shape):
        self.struct = pltpu.VMEM(shape, BF16)


class Leaves:
    def __init__(self, *shape):
        self.struct = pltpu.HBM(shape, BF16)


def only(section, body, *refs):
    @pl.when(lax.axis_index("section") == section)
    def _():
        body(*refs)


def stage(body, outs, smem, *arguments, left=(), scratch=(), grant=16, moved=0):
    spaces = [pltpu.SMEM] * smem + [pltpu.VMEM] * (len(arguments) - smem)
    place = lambda out: pltpu.HBM if isinstance(out, Leaves) else pltpu.VMEM
    out_specs = jax.tree.map(lambda out: pl.BlockSpec(memory_space=place(out)), outs)
    outs = jax.tree.map(lambda out: getattr(out, "struct", out), outs)
    arguments = list(arguments)
    for i in left:
        spaces[i] = pltpu.HBM
        arguments[i] = pltpu.with_memory_space_constraint(arguments[i], pltpu.HBM)
    return pl.pallas_call(
        body,
        out_shape=outs,
        in_specs=[pl.BlockSpec(memory_space=space) for space in spaces],
        out_specs=out_specs,
        scratch_shapes=scratch,
        cost_estimate=pl.CostEstimate(flops=0, bytes_accessed=moved, transcendentals=0) if moved else None,
        compiler_params=pltpu.CompilerParams(vmem_limit_bytes=grant * 1024 * 1024),
    )(*arguments)


def by_kernels(hidden, lengths, text_count, timestep, mod_table, w_qkv, w_out, qk_gain, stale_cache):
    count = lax.axis_size("tok")
    halves = lax.axis_size("fsdp")
    own = lax.axis_index("tok")
    patches, cap_dev, width = hidden.shape
    rows = patches * cap_dev
    total = rows * count
    live = total * 3 // 4
    depth, local_width = w_qkv.shape[1], w_qkv.shape[3]
    pairs = 2
    lines = count // pairs
    line, side = own // pairs, own % pairs
    half_width = local_width // pairs
    groups = math.gcd(half_width // HEAD_DIM, lines)
    turns = lines // groups
    group_width = half_width // groups
    cap_all = cap_dev * count
    dims = Dims(
        count, pairs, patches, cap_dev, cap_all, total, live, depth, groups, turns, group_width
    )
    share = live // turns
    fold = share // 2

    def struct(*shape):
        return jax.ShapeDtypeStruct(shape, BF16)

    kernel = lambda body, *rest: functools.partial(body, dims, *rest)
    working = lambda section, body, *rest: functools.partial(only, section, kernel(body, *rest))
    place = lambda s, f, t: (s * halves + f) * count + t

    def send(block, source, target, df=0, dt=0):
        ends = [
            (place(source, f, t), place(target, f ^ df, t ^ dt))
            for f in range(halves)
            for t in range(count)
        ]
        return lax.ppermute(block, ("section", "fsdp", "tok"), ends)

    def grouped(blocks, section, working, idle):
        sizes = {len(group) for group in working + idle}
        if len(sizes) > 1 or len(working) != len(idle):
            idle = working
        groups = [[place(section, *at) for at in group] for group in working]
        groups += [[place(1 - section, *at) for at in group] for group in idle]
        return lax.all_to_all(
            blocks, ("section", "fsdp", "tok"), 0, 0, axis_index_groups=groups, tiled=False
        )

    def over_tok(blocks, section):
        half = lines // 2
        working = [[(f, t) for t in range(count)] for f in range(halves)]
        idle = [
            [(f, t) for f in range(halves) for t in range(z * pairs, (z + half) * pairs)]
            for z in range(0, lines, half)
        ]
        return grouped(blocks, section, working, idle)

    def over_lines(blocks, section):
        working = [
            [(f, z * pairs + y) for z in range(lines)] for f in range(halves) for y in range(pairs)
        ]
        idle = [
            [(f, z * pairs + y) for f in range(halves) for y in range(pairs)] for z in range(lines)
        ]
        return grouped(blocks, section, working, idle)

    def all_devices(blocks):
        return lax.all_to_all(blocks, ("fsdp", "tok"), 0, 0, tiled=False)

    def after(done, *operands):
        return lax.optimization_barrier((done, *operands))

    height = live + fold
    attended_shape = (
        Leaves(count, fold, 2 * group_width),
        Leaves(total, 2 * group_width),
    )
    attended_scratch = [
        pltpu.VMEM((fold, 2 * group_width), BF16),
        pltpu.VMEM((total, 2 * group_width), BF16),
        pltpu.SemaphoreType.DMA((count + 1,)),
    ]
    weights = w_qkv[0].transpose(1, 0, 2)
    near = w_out[0]
    gains = qk_gain[0]
    stale = lax.dynamic_slice_in_dim(
        stale_cache[0].reshape(2, total, local_width),
        side * half_width + line % groups * group_width,
        group_width,
        2,
    )

    blocks = stage(
        kernel(send_rows),
        Leaves(count, rows, depth + 128),
        0,
        hidden,
        scratch=[pltpu.VMEM((count, rows, depth + 128), BF16), pltpu.SemaphoreType.DMA((count,))],
        grant=62,
    )
    blocks, step, lengths, text_count, weights_now = after(
        blocks, timestep, lengths, text_count, weights
    )
    sizes = jnp.concatenate([lengths, text_count])
    loaded_first = stage(
        working(0, load, False),
        Stays(3, depth, local_width),
        0,
        weights_now,
        left=(0,),
        scratch=[pltpu.SemaphoreType.DMA((3,))],
        moved=4 * weights.size,
    )
    arrived = over_tok(blocks, 0)
    mod = lax.dynamic_slice(
        mod_table[0].transpose(1, 0, 2), (0, step[0], line * pairs * depth), (6, 1, pairs * depth)
    )[:, 0]

    states, blocks = stage(
        working(0, first_partials),
        (struct(live, depth), Leaves(count, height, 2 * group_width)),
        1,
        sizes,
        mod,
        loaded_first,
        arrived,
        scratch=[
            pltpu.VMEM((count, height, 2 * group_width), BF16),
            pltpu.SemaphoreType.DMA((count,)),
        ],
    )
    blocks, weights_now = after(blocks, weights)
    arrived = over_tok(blocks, 0)
    loaded_last = stage(
        working(1, load, True),
        Stays(3, depth, half_width),
        0,
        weights_now,
        left=(0,),
        scratch=[pltpu.SemaphoreType.DMA((3,))],
        moved=4 * weights.size,
    )
    leaving = lax.dynamic_slice_in_dim(weights_now, (1 - side) * half_width, half_width, 2)

    attended, cache_first = stage(
        working(0, attention, 0),
        attended_shape,
        1,
        sizes,
        gains,
        stale,
        arrived,
        scratch=attended_scratch,
    )
    attended, leaving = after(attended, leaving)
    arrived = over_tok(attended, 0)
    swapped_last = send(leaving, 1, 1, dt=1)
    made = stage(
        working(0, layer_rows),
        struct(live, depth),
        1,
        sizes,
        mod,
        near,
        states,
        arrived,
    )
    given = send(made, 0, 1)
    across = send(made, 0, 1, df=1)
    others = send(made, 0, 1, dt=1)
    corner = send(made, 0, 1, df=1, dt=1)
    blocks = stage(
        working(1, next_partials),
        Leaves(lines, height + 16, 2 * group_width),
        1,
        sizes,
        mod,
        loaded_last,
        swapped_last,
        corner,
        others,
        across,
        given,
        scratch=[
            pltpu.VMEM((lines, height + 16, 2 * group_width), BF16),
            pltpu.SemaphoreType.DMA((lines,)),
        ],
    )
    blocks, made, cache_first = after(blocks, made, cache_first)
    arrived = over_lines(blocks, 1)
    back = send(made, 0, 0, df=1)
    side_first = send(cache_first, 0, 0, dt=1)
    arrived, back, side_first = after(arrived, back, side_first)

    attended, cache_last = stage(
        working(1, attention, 1),
        attended_shape,
        1,
        sizes,
        gains,
        stale,
        arrived,
        scratch=attended_scratch,
    )
    arrived = over_tok(attended, 1)
    side_last = send(cache_last, 1, 1, dt=1)
    arrived, side_last = after(arrived, side_last)
    blocks, pair, kept_pair = stage(
        kernel(last_rows),
        (
            Leaves(halves * count, rows, depth),
            Leaves(2, total, 2 * group_width),
            Stays(2, total, 2 * group_width),
        ),
        1,
        sizes,
        mod,
        near,
        made,
        back,
        given,
        across,
        cache_first,
        cache_last,
        side_first,
        side_last,
        arrived,
        left=(7, 8),
        scratch=[
            pltpu.VMEM((count, rows, depth), BF16),
            pltpu.SemaphoreType.DMA((halves,)),
            pltpu.SemaphoreType.DMA,
            pltpu.SemaphoreType.DMA,
        ],
    )
    arrived = all_devices(blocks)
    other = lax.ppermute(pair, "tok", [(t, t ^ pairs) for t in range(count)])
    final, new_cache = stage(
        kernel(join),
        (struct(1, patches, cap_dev, width), struct(2, total, local_width)),
        0,
        arrived,
        kept_pair,
        other,
        scratch=[pltpu.VMEM((groups * pairs, total, 2 * group_width), BF16)],
    )
    return final, new_cache.reshape(1, 2, patches, cap_all, local_width)


def solution(mesh):
    in_specs = (
        P(None, "tok", None),
        P(),
        P(),
        P(),
        P("section", None, None, None),
        P("section", "tok", None, "fsdp"),
        P("section", "tok", "fsdp"),
        P("section", None, None),
        P("section", None, None, None, "fsdp"),
    )
    out_specs = (P("section", None, "tok", None), P("section", None, None, None, "fsdp"))
    local = by_kernels if mesh.shape["tok"] <= MOST_PEERS else by_all_to_all
    return jax.shard_map(local, mesh=mesh, in_specs=in_specs, out_specs=out_specs, check_vma=False)
```

```python
import collections
import functools
import math

import jax
import jax.numpy as jnp
from jax import lax
from jax.experimental import pallas as pl
from jax.experimental.pallas import tpu as pltpu
from jax.sharding import PartitionSpec as P

HEAD_DIM = 64
F32 = jnp.float32
BF16 = jnp.bfloat16
MOST_PEERS = 8


def swap(block, axis):
    size = lax.axis_size(axis)
    return lax.ppermute(block, axis, [(i, size - 1 - i) for i in range(size)])


def exchange(blocks):
    return lax.all_to_all(blocks, "tok", 0, 0, tiled=False)


def gather(block):
    count = lax.axis_size("tok")
    return exchange(jnp.broadcast_to(block[None], (count,) + block.shape))


def layer_norm(values, eps):
    mean = jnp.mean(values, axis=-1, keepdims=True)
    centred = values - mean
    spread = jnp.mean(centred * centred, axis=-1, keepdims=True)
    return centred * lax.rsqrt(spread + eps)


def three_terms(values):
    high = lax.reduce_precision(values, 8, 7)
    rest = values - high
    middle = lax.reduce_precision(rest, 8, 7)
    return jnp.concatenate([high, middle, rest - middle], axis=-1).astype(BF16)


def from_three(terms):
    terms = terms.astype(F32)
    count = terms.shape[-1] // 3
    return terms[..., :count] + terms[..., count : 2 * count] + terms[..., 2 * count :]


def by_all_to_all(hidden, lengths, text_count, timestep, mod_table, w_qkv, w_out, qk_gain, stale_cache):
    first = lax.axis_index("section") == 0
    own_half = lax.axis_index("section")
    tok_count = lax.axis_size("tok")
    tok_index = lax.axis_index("tok")
    patches, cap_dev, width = hidden.shape
    rows = patches * cap_dev
    total = rows * tok_count
    depth = w_qkv.shape[1]
    half = w_qkv.shape[3] // 2
    heads = half // HEAD_DIM

    def both_layers(own, other):
        return jnp.where(first, own, other), jnp.where(first, other, own)

    def halves(array):
        axis = array.ndim - 1
        keep = lax.dynamic_slice_in_dim(array, own_half * half, half, axis)
        send = lax.dynamic_slice_in_dim(array, (1 - own_half) * half, half, axis)
        return both_layers(keep, swap(send, "section"))

    offsets = jnp.cumsum(lengths) - lengths
    row = jnp.arange(total, dtype=jnp.int32)
    row_patch = (row // cap_dev) % patches
    row_slot = (row // rows) * cap_dev + row % cap_dev
    row_live = row_slot < lengths[row_patch]
    is_text = ((offsets[row_patch] + row_slot) < text_count[0])[:, None]
    own_patch = jnp.arange(rows, dtype=jnp.int32) // cap_dev
    own_live = (tok_index * cap_dev + jnp.arange(rows, dtype=jnp.int32) % cap_dev) < lengths[own_patch]
    cap_all = cap_dev * tok_count
    stale_patch = jnp.arange(patches * cap_all, dtype=jnp.int32) // cap_all
    stale_live = (jnp.arange(patches * cap_all, dtype=jnp.int32) % cap_all) < lengths[stale_patch]
    fresh_seen = row_live[None, :] & (row_patch[None, :] <= own_patch[:, None])
    stale_seen = stale_live[None, :] & (stale_patch[None, :] > own_patch[:, None])
    seen = jnp.concatenate([fresh_seen, stale_seen], axis=1)

    states = hidden.reshape(rows, width).astype(F32)
    mean = jnp.mean(states, axis=-1, keepdims=True)
    centred = states - mean
    inverse = lax.rsqrt(jnp.mean(centred * centred, axis=-1, keepdims=True) + 1e-05)
    stats = three_terms(jnp.concatenate([mean, inverse], axis=-1))
    stats = jnp.pad(stats, ((0, 0), (0, 128 - stats.shape[1])))
    blocks = hidden.reshape(rows, tok_count, depth).transpose(1, 0, 2)
    blocks = jnp.concatenate(
        [blocks, jnp.broadcast_to(stats[None], (tok_count,) + stats.shape)], axis=-1
    )
    arrived = exchange(blocks).reshape(total, depth + 128)
    slices = arrived[:, :depth].astype(F32)
    stats = from_three(arrived[:, depth : depth + 6])

    weight_in = halves(w_qkv[0].transpose(1, 0, 2))
    weight_out = halves(w_out[0])
    stale = halves(stale_cache[0].reshape(2, patches * cap_all, 2 * half))
    modulation = lax.dynamic_index_in_dim(mod_table[0], timestep[0], 0, keepdims=False)
    modulation = lax.dynamic_slice_in_dim(modulation, tok_index * depth, depth, 1)
    modulation = both_layers(modulation, swap(modulation, "section"))
    gains = both_layers(qk_gain[0], swap(qk_gain[0], "section"))

    outputs, caches = [], []
    for layer in range(2):
        if layer:
            part_mean = jnp.mean(slices, axis=-1, keepdims=True)
            off = slices - part_mean
            part = jnp.concatenate([part_mean, jnp.sum(off * off, axis=-1, keepdims=True)], axis=-1)
            parts = gather(part)
            mean = jnp.mean(parts[..., 0], axis=0)
            apart = parts[..., 0] - mean[None]
            spread = jnp.sum(parts[..., 1] + depth * apart * apart, axis=0) / (depth * tok_count)
            stats = jnp.stack([mean, lax.rsqrt(spread + 1e-05)], axis=-1)
        mod = modulation[layer].astype(F32)
        shift = jnp.where(is_text, mod[3], mod[0])
        scale = jnp.where(is_text, mod[4], mod[1])
        gate = jnp.where(is_text, mod[5], mod[2])
        normed = (slices - stats[:, :1]) * stats[:, 1:]
        modded = (normed * (1.0 + scale) + shift).astype(BF16)
        partial = jnp.concatenate(
            [
                jnp.dot(modded, weight_in[layer][i], preferred_element_type=F32).astype(BF16)
                for i in range(3)
            ],
            axis=-1,
        ).reshape(tok_count, rows, 3 * half)
        mixed = jnp.sum(exchange(partial).astype(F32), axis=0).reshape(rows, 3, heads, HEAD_DIM)
        gain = gains[layer]
        queries = (layer_norm(mixed[:, 0], 1e-06) * gain[0]).astype(BF16)
        keys_new = (layer_norm(mixed[:, 1], 1e-06) * gain[1]).astype(BF16)
        fresh = jnp.stack([keys_new, mixed[:, 2].astype(BF16)])
        fresh = jnp.where(own_live[None, :, None, None], fresh, jnp.zeros_like(fresh))
        fresh = gather(fresh.reshape(2, rows, half))
        caches.append(fresh)
        fresh = fresh.transpose(1, 0, 2, 3).reshape(2, total, half)
        keys_values = jnp.concatenate([fresh, stale[layer]], axis=1).reshape(
            2, total + patches * cap_all, heads, HEAD_DIM
        )
        scores = (
            jnp.einsum("qhd,khd->hqk", queries, keys_values[0], preferred_element_type=F32)
            * HEAD_DIM ** (-0.5)
        )
        scores = jnp.where(seen[None], scores, -jnp.inf)
        expo = jnp.exp(scores - jnp.max(scores, axis=-1, keepdims=True))
        weights = (expo / jnp.sum(expo, axis=-1, keepdims=True)).astype(BF16)
        attended = jnp.einsum("hqk,khd->qhd", weights, keys_values[1], preferred_element_type=F32)
        attended = gather(attended.astype(BF16).reshape(rows, half)).reshape(total, half)
        projected = lax.dot_general(
            attended, weight_out[layer], (((1,), (1,)), ((), ())), preferred_element_type=F32
        ).astype(BF16)
        projected = projected.astype(F32) + swap(projected, "section").astype(F32)
        projected = projected.astype(BF16)
        projected = projected.astype(F32) + swap(projected, "fsdp").astype(F32)
        result = jnp.where(row_live[:, None], slices + gate * projected, 0.0).astype(BF16)
        outputs.append(result)
        slices = result.astype(F32)

    final = jnp.where(first, outputs[0], outputs[1]).reshape(tok_count, rows, depth)
    final = exchange(final).transpose(1, 0, 2).reshape(1, patches, cap_dev, width)
    mine = jnp.where(first, caches[0], caches[1])
    theirs = swap(jnp.where(first, caches[1], caches[0]), "section")
    cache = jnp.concatenate(
        [jnp.where(first, mine, theirs), jnp.where(first, theirs, mine)], axis=-1
    ).reshape(tok_count, 2, patches, cap_dev, 2 * half)
    cache = cache.transpose(1, 2, 0, 3, 4).reshape(1, 2, patches, cap_all, 2 * half)
    return final, cache


def iota(shape, dim):
    return lax.broadcasted_iota(jnp.int32, shape, dim)


def total_of(parts):
    total = parts[0]
    for part in parts[1:]:
        total = total + part
    return total


def split_three(value):
    high = value.astype(BF16).astype(F32)
    middle = (value - high).astype(BF16).astype(F32)
    return [high, middle, value - high - middle]


def in_lanes(columns, lanes):
    rows = columns[0].shape[0]
    lane = iota((rows, lanes), 1)
    block = jnp.zeros((rows, lanes), F32)
    for i, column in enumerate(columns):
        block = jnp.where(lane == i, column, block)
    return block.astype(BF16)


def from_columns(block, at):
    return [
        sum(block[:, at + i : at + i + 1] for i in range(3 * j, 3 * j + 3)) for j in range(2)
    ]


def bounds(sizes, patches):
    ends = [sizes[0]]
    for p in range(1, patches):
        ends.append(ends[-1] + sizes[p])
    return ends


def positions(sizes, patch, slot, patches):
    ends = bounds(sizes, patches)
    position = jnp.full(slot.shape, -1, jnp.int32)
    for p in range(patches):
        own = (patch == p) & (slot < sizes[p])
        position = jnp.where(own, slot + (ends[p] - sizes[p]), position)
    return position


def slots_by_device(shape, dim, cap_dev, patches):
    index = iota(shape, dim)
    rows = cap_dev * patches
    return (index // cap_dev) % patches, (index // rows) * cap_dev + index % cap_dev


def slots_by_patch(shape, dim, cap_all):
    index = iota(shape, dim)
    return index // cap_all, index % cap_all


def begin(source, target, sem):
    copy = pltpu.make_async_copy(source, target, sem)
    copy.start()
    return copy


def finish(copies):
    for copy in copies:
        copy.wait()


def send_rows(dims, hidden, out, staged, sems):
    rows = dims.patches * dims.cap_dev
    given = hidden[...].astype(F32).reshape(rows, hidden.shape[2])
    mean = jnp.mean(given, axis=-1, keepdims=True)
    centred = given - mean
    inverse = lax.rsqrt(jnp.mean(centred * centred, axis=-1, keepdims=True) + 1e-05)
    stats = in_lanes(split_three(mean) + split_three(inverse), 128)
    given = given.astype(BF16)
    copies = []
    for i in range(dims.count):
        staged[i, :, : dims.depth] = given[:, i * dims.depth : (i + 1) * dims.depth]
        staged[i, :, dims.depth :] = stats
        copies.append(begin(staged.at[i], out.at[i], sems.at[i]))
    finish(copies)


def modulation_rows(dims, mod, sizes):
    is_text = iota((dims.live, 1), 0) < sizes[dims.patches]
    mod = mod[...].astype(F32)
    return [
        jnp.where(is_text, mod[i + 3 : i + 4, :], mod[i : i + 1, :]) for i in range(3)
    ]


def put_partials(dims, out, staged, sems, query, key, value, extra, stats):
    live, width, groups, turns = dims.live, dims.group_width, dims.groups, dims.turns
    share = live // turns
    fold = share // 2
    sides = query.shape[1] // (groups * width)
    copies = []
    for g in range(sides * groups):
        cut = slice(g * width, (g + 1) * width)
        pair = jnp.concatenate([key[:live, cut], value[:live, cut]], axis=1).astype(BF16)
        if extra:
            last = query[live : live + 4, cut]
            rest = [
                jnp.concatenate([key[live : live + 4, cut], value[live : live + 4, cut]], axis=1),
                jnp.concatenate([last, jnp.zeros_like(last)], axis=1),
            ]
        else:
            rest = []
        for h in range(turns):
            part = query[h * share : (h + 1) * share, cut]
            rows = [jnp.concatenate([part[:fold], part[fold:]], axis=1)] + rest
            at = (h * groups + g % groups) * sides + g // groups
            staged[at, :live, :] = pair
            rows = jnp.concatenate(rows, axis=0)
            staged[at, live : live + rows.shape[0], :] = rows.astype(BF16)
            if extra:
                staged[at, live + fold + 8 :, :] = stats
            copies.append(begin(staged.at[at], out.at[at], sems.at[at]))
    finish(copies)


def own_then_other(dims, wide):
    second = lax.axis_index("tok") % dims.pairs == 1
    left, right = wide[:, : dims.depth], wide[:, dims.depth :]
    return jnp.where(second, right, left), jnp.where(second, left, right)


def load(dims, side, weights, out, sems):
    columns = out.shape[2]
    start = pl.multiple_of(lax.axis_index("tok") % dims.pairs * columns, 128) if side else 0
    finish(
        [
            begin(weights.at[i, :, pl.ds(start, columns)], out.at[i], sems.at[i])
            for i in range(out.shape[0])
        ]
    )


def first_partials(
    dims, sizes, mod, weights, values, arrived, kept_states, out, held, sem, staged, sems
):
    copy = begin(values.at[2], held, sem)
    patch, slot = slots_by_device((1, dims.total), 1, dims.cap_dev, dims.patches)
    position = positions(sizes, patch, slot, dims.patches)
    pick = (iota((dims.live, dims.total), 0) == position).astype(F32).astype(BF16)
    rows = arrived[...].reshape(dims.total, dims.depth + 128)
    states = jnp.dot(pick, rows, preferred_element_type=F32)
    mean, inverse = from_columns(states, dims.depth)
    states = states[:, : dims.depth]
    own_mod = own_then_other(dims, mod[...].astype(F32))[0]
    shift, scale, gate = modulation_rows(dims, own_mod, sizes)
    modded = ((states - mean) * inverse * (1.0 + scale) + shift).astype(BF16)
    kept_states[...] = states.astype(BF16)
    mixed = [jnp.dot(modded, weights[i], preferred_element_type=F32) for i in range(2)]
    copy.wait()
    mixed.append(jnp.dot(modded, held[...], preferred_element_type=F32))
    put_partials(dims, out, staged, sems, *mixed, False, None)


def head_means(values, blocks, terms):
    total = None
    for _ in range(terms):
        term = values.astype(BF16)
        part = jnp.dot(term, blocks, preferred_element_type=F32)
        total = part if total is None else total + part
        values = values - term.astype(F32)
    return total * (1.0 / HEAD_DIM)


def head_norm(values, gain, blocks):
    centred = values - head_means(values, blocks, 3)
    spread = head_means(centred * centred, blocks, 2)
    return (centred * lax.rsqrt(spread + 1e-06) * gain).astype(BF16)


def own_share(dims, turn, value, share):
    part = value[:share]
    for h in range(1, dims.turns):
        part = jnp.where(turn == h, value[h * share : (h + 1) * share], part)
    return part


def attention(
    dims, layer, sizes, gains, stale, arrived, attended, cache, fresh_rows, block, sems
):
    count = arrived.shape[0]
    turn = lax.axis_index("tok") // dims.pairs // dims.groups
    live, width = dims.live, dims.group_width
    share = live // dims.turns
    fold = share // 2
    pairs = total_of([arrived[i, :live, :].astype(F32) for i in range(count)])
    height = fold + 8 if layer else fold
    folded = [arrived[i, live : live + height, :].astype(F32) for i in range(count)]
    extras = [part[fold:] for part in folded]
    folded = total_of(folded)
    queries = jnp.concatenate([folded[:fold, :width], folded[:fold, width:]], axis=0)
    if layer:
        is_text = iota((live, 1), 0) < sizes[dims.patches]
        eye = (iota((live, live), 0) == iota((live, live), 1)).astype(F32).astype(BF16)
        means, spreads = [], []
        stats = jnp.concatenate(
            [arrived[i, live + fold + 8 :, :live].astype(F32) for i in range(count)], axis=0
        )
        columns = lax.dot_general(
            eye, stats.astype(BF16), (((1,), (1,)), ((), ())), preferred_element_type=F32
        )
        for i in range(count):
            mean, spread = from_columns(columns, 8 * i)
            means.append(mean)
            spreads.append(spread)
        mean = total_of(means) * (1.0 / count)
        apart = [part - mean for part in means]
        spread = total_of(spreads) + dims.count // count * dims.depth * total_of([part * part for part in apart])
        inverse = lax.rsqrt(spread * (1.0 / (dims.count * dims.depth)) + 1e-05)
        pairs = pairs + total_of(
            [a * jnp.where(is_text, e[0:1], e[1:2]) for a, e in zip(apart, extras)]
        )
        total = total_of(extras)
        pairs = pairs * inverse + jnp.where(is_text, total[2:3], total[3:4])
        mine = functools.partial(own_share, dims, turn, share=share)
        text_mine = (iota((share, 1), 0) + turn * share) < sizes[dims.patches]
        queries = queries + total_of(
            [
                mine(a) * jnp.where(text_mine, e[4:5, :width], e[5:6, :width])
                for a, e in zip(apart, extras)
            ]
        )
        queries = queries * mine(inverse) + jnp.where(text_mine, total[6:7, :width], total[7:8, :width])
    ends = bounds(sizes, dims.patches)
    query_at = iota((share, 1), 0) + turn * share
    query_patch = jnp.zeros((share, 1), jnp.int32)
    for end in ends[:-1]:
        query_patch = query_patch + (query_at >= end).astype(jnp.int32)
    query_end = jnp.zeros((share, 1), jnp.int32)
    for p, end in enumerate(ends):
        query_end = jnp.where(query_patch == p, end, query_end)
    stale_patch, stale_slot = slots_by_patch((1, dims.total), 1, dims.cap_all)
    stale_live = positions(sizes, stale_patch, stale_slot, dims.patches) >= 0
    fresh_seen = iota((share, live), 1) < query_end
    stale_seen = stale_live & (stale_patch > query_patch)
    heads = width // HEAD_DIM
    contract = (((1,), (1,)), ((), ()))
    same = iota((width, width), 0) // HEAD_DIM == iota((width, width), 1) // HEAD_DIM
    blocks = same.astype(F32).astype(BF16)
    gain = [jnp.concatenate([gains[i : i + 1, :]] * heads, axis=1) for i in range(2)]
    query = head_norm(queries, gain[0], blocks).astype(F32)
    key = head_norm(pairs[:, :width], gain[1], blocks)
    value = pairs[:, width:].astype(BF16)
    lanes = iota((heads * share, width), 1) // HEAD_DIM == iota((heads * share, width), 0) // share
    stacked = jnp.where(lanes, jnp.concatenate([query] * heads, axis=0), 0.0).astype(BF16)
    fresh = lax.dot_general(stacked, key, contract, preferred_element_type=F32)
    old = lax.dot_general(stacked, stale[0], contract, preferred_element_type=F32)
    repeated = lambda seen: jnp.concatenate([seen.astype(jnp.int32)] * heads, axis=0) > 0
    fresh = jnp.where(repeated(fresh_seen), fresh * HEAD_DIM ** (-0.5), -jnp.inf)
    old = jnp.where(repeated(stale_seen), old * HEAD_DIM ** (-0.5), -jnp.inf)
    top = jnp.maximum(jnp.max(fresh, axis=-1, keepdims=True), jnp.max(old, axis=-1, keepdims=True))
    fresh, old = jnp.exp(fresh - top), jnp.exp(old - top)
    norm = jnp.sum(fresh, axis=-1, keepdims=True) + jnp.sum(old, axis=-1, keepdims=True)
    fresh, old = (fresh / norm).astype(BF16), (old / norm).astype(BF16)
    outs = jnp.dot(fresh, value, preferred_element_type=F32)
    outs = outs + jnp.dot(old, stale[1], preferred_element_type=F32)
    outs = jnp.where(lanes, outs, 0.0)
    outs = total_of([outs[h * share : (h + 1) * share] for h in range(heads)])
    block[...] = jnp.concatenate([outs[:fold], outs[fold:]], axis=1).astype(BF16)
    copies = [begin(block, attended.at[i], sems.at[i]) for i in range(attended.shape[0])]
    new = jnp.concatenate([key.astype(F32), pairs[:, width:]], axis=1).astype(BF16)
    patch, slot = slots_by_patch((dims.total, 1), 0, dims.cap_all)
    position = positions(sizes, patch, slot, dims.patches)
    spread_out = (iota((dims.total, live), 1) == position).astype(F32).astype(BF16)
    fresh_rows[...] = jnp.dot(spread_out, new, preferred_element_type=F32).astype(BF16)
    copies.append(begin(fresh_rows, cache, sems.at[attended.shape[0]]))
    finish(copies)


def output_rows(dims, sizes, mod, near, states, arrived):
    width = dims.group_width
    rows = []
    for h in range(dims.turns):
        parts = [
            arrived[(h * dims.groups + g) * dims.pairs + y].astype(F32)
            for y in range(dims.pairs)
            for g in range(dims.groups)
        ]
        rows.append(jnp.concatenate([part[:, :width] for part in parts], axis=1))
        rows.append(jnp.concatenate([part[:, width:] for part in parts], axis=1))
    heads = jnp.concatenate(rows, axis=0).astype(BF16)
    projected = lax.dot_general(
        heads, near[...], (((1,), (1,)), ((), ())), preferred_element_type=F32
    )
    gate = own_then_other(dims, modulation_rows(dims, mod, sizes)[2])[0]
    return (from_first(dims, states) + gate * projected).astype(BF16)


def from_first(dims, states):
    half = jnp.zeros((dims.live, 1), jnp.int32) + lax.axis_index("fsdp")
    return jnp.where(half == 0, states.astype(F32), 0.0)


def layer_rows(dims, sizes, mod, near, states, arrived, out):
    out[...] = output_rows(dims, sizes, mod, near, states[...], arrived)


def both(first, second):
    return (first[...].astype(F32) + second[...].astype(F32)).astype(BF16)


def next_partials(
    dims, sizes, mod, weights, swapped, corner, others, across, given, out, staged, sems
):
    states = [both(given, across), both(others, corner)]
    states = jnp.concatenate([part.astype(F32) for part in states], axis=1)
    mean = jnp.mean(states, axis=-1, keepdims=True)
    centred = states - mean
    spread = jnp.sum(centred * centred, axis=-1, keepdims=True)
    stats = in_lanes(split_three(mean) + split_three(spread), 128)
    eye = (iota((dims.live, dims.live), 0) == iota((dims.live, dims.live), 1)).astype(F32).astype(BF16)
    stats = lax.dot_general(stats, eye, (((0,), (0,)), ((), ())), preferred_element_type=F32)[:8]
    lanes = 2 * dims.group_width
    stats = jnp.concatenate([stats, jnp.zeros((8, lanes - dims.live), F32)], axis=1).astype(BF16)
    rows = jnp.concatenate(own_then_other(dims, mod[...].astype(F32)), axis=1)
    is_text = iota((dims.live, 1), 0) < sizes[dims.patches]
    scaled = centred * (1.0 + jnp.where(is_text, rows[4:5], rows[1:2]))
    extra = jnp.concatenate(
        [1.0 + rows[4:5], 1.0 + rows[1:2], rows[3:4], rows[0:1], jnp.zeros_like(rows[:4])], axis=0
    )
    left = jnp.concatenate([scaled, extra], axis=0).astype(BF16)
    mixed = [
        jnp.dot(left[:, : dims.depth], weights[i], preferred_element_type=F32)
        + jnp.dot(left[:, dims.depth :], swapped[i], preferred_element_type=F32)
        for i in range(3)
    ]
    put_partials(dims, out, staged, sems, *mixed, True, stats)


def last_rows(
    dims, sizes, mod, near, made, back, given, across, first_cache, last_cache, first_side,
    last_side, arrived, out, pair, pieces, staged, sems, fetched, sent
):
    def spread(states):
        patch, slot = slots_by_device((dims.total, 1), 0, dims.cap_dev, dims.patches)
        position = positions(sizes, patch, slot, dims.patches)
        pick = (iota((dims.total, dims.live), 1) == position).astype(F32).astype(BF16)
        blocks = jnp.dot(pick, states, preferred_element_type=F32).astype(BF16)
        staged[...] = blocks.reshape(staged.shape)
        finish(
            [
                begin(staged, out.at[pl.ds(i * dims.count, dims.count)], sems.at[i])
                for i in range(out.shape[0] // dims.count)
            ]
        )

    section = lax.axis_index("section")

    @pl.when(section == 0)
    def _():
        copy = begin(first_cache, pieces.at[0], fetched)
        pieces[1] = first_side[...]
        copy.wait()
        copy = begin(pieces, pair, sent)
        states = from_first(dims, both(made, back)).astype(BF16)
        spread(states)
        copy.wait()

    @pl.when(section != 0)
    def _():
        pieces[0] = last_cache[...]
        pieces[1] = last_side[...]
        copy = begin(pieces, pair, sent)
        states = output_rows(dims, sizes, mod, near, both(given, across), arrived)
        spread(states)
        copy.wait()


def join(dims, arrived, pair, other, out, cache, pieces):
    for i in range(dims.count):
        block = arrived[i].astype(F32) + arrived[dims.count + i].astype(F32)
        block = block.reshape(dims.patches, dims.cap_dev, dims.depth)
        out[0, :, :, i * dims.depth : (i + 1) * dims.depth] = block.astype(BF16)
    groups, width, pairs = dims.groups, dims.group_width, dims.pairs
    own = lax.axis_index("tok")
    line, side = own // pairs, own % pairs
    for g, blocks in enumerate((pair, other)):
        for y in range(pairs):
            pieces[(side ^ y) * groups + (line % groups ^ g)] = blocks[y]
    for i in range(2):
        cut = slice(i * width, (i + 1) * width)
        cache[i] = jnp.concatenate([pieces[j][:, cut] for j in range(groups * pairs)], axis=1)


Dims = collections.namedtuple(
    "Dims",
    [
        "count",
        "pairs",
        "patches",
        "cap_dev",
        "cap_all",
        "total",
        "live",
        "depth",
        "groups",
        "turns",
        "group_width",
    ],
)


class Stays:
    def __init__(self, *shape):
        self.struct = pltpu.VMEM(shape, BF16)


class Leaves:
    def __init__(self, *shape):
        self.struct = pltpu.HBM(shape, BF16)


def only(section, body, *refs):
    @pl.when(lax.axis_index("section") == section)
    def _():
        body(*refs)


def stage(body, outs, smem, *arguments, left=(), scratch=(), grant=16, moved=0):
    spaces = [pltpu.SMEM] * smem + [pltpu.VMEM] * (len(arguments) - smem)
    place = lambda out: pltpu.HBM if isinstance(out, Leaves) else pltpu.VMEM
    out_specs = jax.tree.map(lambda out: pl.BlockSpec(memory_space=place(out)), outs)
    outs = jax.tree.map(lambda out: getattr(out, "struct", out), outs)
    arguments = list(arguments)
    for i in left:
        spaces[i] = pltpu.HBM
        arguments[i] = pltpu.with_memory_space_constraint(arguments[i], pltpu.HBM)
    return pl.pallas_call(
        body,
        out_shape=outs,
        in_specs=[pl.BlockSpec(memory_space=space) for space in spaces],
        out_specs=out_specs,
        scratch_shapes=scratch,
        cost_estimate=pl.CostEstimate(flops=0, bytes_accessed=moved, transcendentals=0) if moved else None,
        compiler_params=pltpu.CompilerParams(vmem_limit_bytes=grant * 1024 * 1024),
    )(*arguments)


def by_kernels(hidden, lengths, text_count, timestep, mod_table, w_qkv, w_out, qk_gain, stale_cache):
    count = lax.axis_size("tok")
    halves = lax.axis_size("fsdp")
    own = lax.axis_index("tok")
    patches, cap_dev, width = hidden.shape
    rows = patches * cap_dev
    total = rows * count
    live = total * 3 // 4
    depth, local_width = w_qkv.shape[1], w_qkv.shape[3]
    pairs = 2
    lines = count // pairs
    line, side = own // pairs, own % pairs
    half_width = local_width // pairs
    groups = math.gcd(half_width // HEAD_DIM, lines)
    turns = lines // groups
    group_width = half_width // groups
    cap_all = cap_dev * count
    dims = Dims(
        count, pairs, patches, cap_dev, cap_all, total, live, depth, groups, turns, group_width
    )
    share = live // turns
    fold = share // 2

    def struct(*shape):
        return jax.ShapeDtypeStruct(shape, BF16)

    kernel = lambda body, *rest: functools.partial(body, dims, *rest)
    working = lambda section, body, *rest: functools.partial(only, section, kernel(body, *rest))
    place = lambda s, f, t: (s * halves + f) * count + t

    def send(block, source, target, df=0, dt=0):
        ends = [
            (place(source, f, t), place(target, f ^ df, t ^ dt))
            for f in range(halves)
            for t in range(count)
        ]
        return lax.ppermute(block, ("section", "fsdp", "tok"), ends)

    def grouped(blocks, section, working, idle):
        sizes = {len(group) for group in working + idle}
        if len(sizes) > 1 or len(working) != len(idle):
            idle = working
        groups = [[place(section, *at) for at in group] for group in working]
        groups += [[place(1 - section, *at) for at in group] for group in idle]
        return lax.all_to_all(
            blocks, ("section", "fsdp", "tok"), 0, 0, axis_index_groups=groups, tiled=False
        )

    def over_tok(blocks, section):
        half = lines // 2
        working = [[(f, t) for t in range(count)] for f in range(halves)]
        idle = [
            [(f, t) for f in range(halves) for t in range(z * pairs, (z + half) * pairs)]
            for z in range(0, lines, half)
        ]
        return grouped(blocks, section, working, idle)

    def over_lines(blocks, section):
        working = [
            [(f, z * pairs + y) for z in range(lines)] for f in range(halves) for y in range(pairs)
        ]
        idle = [
            [(f, z * pairs + y) for f in range(halves) for y in range(pairs)] for z in range(lines)
        ]
        return grouped(blocks, section, working, idle)

    def all_devices(blocks):
        return lax.all_to_all(blocks, ("fsdp", "tok"), 0, 0, tiled=False)

    def after(done, *operands):
        return lax.optimization_barrier((done, *operands))

    height = live + fold
    attended_shape = (
        Leaves(count, fold, 2 * group_width),
        Leaves(total, 2 * group_width),
        Stays(total, 2 * group_width),
    )
    attended_scratch = [
        pltpu.VMEM((fold, 2 * group_width), BF16),
        pltpu.SemaphoreType.DMA((count + 1,)),
    ]
    weights = w_qkv[0].transpose(1, 0, 2)
    near = w_out[0]
    gains = qk_gain[0]
    stale = lax.dynamic_slice_in_dim(
        stale_cache[0].reshape(2, total, local_width),
        side * half_width + line % groups * group_width,
        group_width,
        2,
    )

    blocks = stage(
        kernel(send_rows),
        Leaves(count, rows, depth + 128),
        0,
        hidden,
        scratch=[pltpu.VMEM((count, rows, depth + 128), BF16), pltpu.SemaphoreType.DMA((count,))],
        grant=62,
    )
    blocks, step, lengths, text_count, weights_now = after(
        blocks, timestep, lengths, text_count, weights
    )
    sizes = jnp.concatenate([lengths, text_count])
    loaded_first = stage(
        working(0, load, False),
        Stays(2, depth, local_width),
        0,
        weights_now,
        left=(0,),
        scratch=[pltpu.SemaphoreType.DMA((2,))],
        moved=4 * weights.size,
    )
    arrived = over_tok(blocks, 0)
    mod = lax.dynamic_slice(
        mod_table[0].transpose(1, 0, 2), (0, step[0], line * pairs * depth), (6, 1, pairs * depth)
    )[:, 0]

    states, blocks = stage(
        working(0, first_partials),
        (struct(live, depth), Leaves(count, height, 2 * group_width)),
        1,
        sizes,
        mod,
        loaded_first,
        weights,
        arrived,
        left=(3,),
        scratch=[
            pltpu.VMEM((depth, local_width), BF16),
            pltpu.SemaphoreType.DMA,
            pltpu.VMEM((count, height, 2 * group_width), BF16),
            pltpu.SemaphoreType.DMA((count,)),
        ],
    )
    blocks, weights_now = after(blocks, weights)
    arrived = over_tok(blocks, 0)
    loaded_last = stage(
        working(1, load, True),
        Stays(3, depth, half_width),
        0,
        weights_now,
        left=(0,),
        scratch=[pltpu.SemaphoreType.DMA((3,))],
        moved=4 * weights.size,
    )
    leaving = lax.dynamic_slice_in_dim(weights_now, (1 - side) * half_width, half_width, 2)
    swapped_last = send(leaving, 1, 1, dt=1)
    arrived, swapped_last = after(arrived, swapped_last)

    attended, cache_first, _ = stage(
        working(0, attention, 0),
        attended_shape,
        1,
        sizes,
        gains,
        stale,
        arrived,
        scratch=attended_scratch,
    )
    arrived = over_tok(attended, 0)
    made = stage(
        working(0, layer_rows),
        struct(live, depth),
        1,
        sizes,
        mod,
        near,
        states,
        arrived,
    )
    given = send(made, 0, 1)
    across = send(made, 0, 1, df=1)
    others = send(made, 0, 1, dt=1)
    corner = send(made, 0, 1, df=1, dt=1)
    blocks = stage(
        working(1, next_partials),
        Leaves(lines, height + 16, 2 * group_width),
        1,
        sizes,
        mod,
        loaded_last,
        swapped_last,
        corner,
        others,
        across,
        given,
        scratch=[
            pltpu.VMEM((lines, height + 16, 2 * group_width), BF16),
            pltpu.SemaphoreType.DMA((lines,)),
        ],
    )
    blocks, made, cache_first = after(blocks, made, cache_first)
    arrived = over_lines(blocks, 1)
    back = send(made, 0, 0, df=1)
    side_first = send(cache_first, 0, 0, dt=1)
    arrived, back, side_first = after(arrived, back, side_first)

    attended, cache_last, kept_last = stage(
        working(1, attention, 1),
        attended_shape,
        1,
        sizes,
        gains,
        stale,
        arrived,
        scratch=attended_scratch,
    )
    arrived = over_tok(attended, 1)
    side_last = send(cache_last, 1, 1, dt=1)
    arrived, side_last = after(arrived, side_last)
    blocks, pair, kept_pair = stage(
        kernel(last_rows),
        (
            Leaves(halves * count, rows, depth),
            Leaves(2, total, 2 * group_width),
            Stays(2, total, 2 * group_width),
        ),
        1,
        sizes,
        mod,
        near,
        made,
        back,
        given,
        across,
        cache_first,
        kept_last,
        side_first,
        side_last,
        arrived,
        left=(7,),
        scratch=[
            pltpu.VMEM((count, rows, depth), BF16),
            pltpu.SemaphoreType.DMA((halves,)),
            pltpu.SemaphoreType.DMA,
            pltpu.SemaphoreType.DMA,
        ],
    )
    arrived = all_devices(blocks)
    other = lax.ppermute(pair, "tok", [(t, t ^ pairs) for t in range(count)])
    final, new_cache = stage(
        kernel(join),
        (struct(1, patches, cap_dev, width), struct(2, total, local_width)),
        0,
        arrived,
        kept_pair,
        other,
        scratch=[pltpu.VMEM((groups * pairs, total, 2 * group_width), BF16)],
    )
    return final, new_cache.reshape(1, 2, patches, cap_all, local_width)


def solution(mesh):
    in_specs = (
        P(None, "tok", None),
        P(),
        P(),
        P(),
        P("section", None, None, None),
        P("section", "tok", None, "fsdp"),
        P("section", "tok", "fsdp"),
        P("section", None, None),
        P("section", None, None, None, "fsdp"),
    )
    out_specs = (P("section", None, "tok", None), P("section", None, None, None, "fsdp"))
    local = by_kernels if mesh.shape["tok"] <= MOST_PEERS else by_all_to_all
    return jax.shard_map(local, mesh=mesh, in_specs=in_specs, out_specs=out_specs, check_vma=False)
```

```python
import collections
import functools
import math

import jax
import jax.numpy as jnp
from jax import lax
from jax.experimental import pallas as pl
from jax.experimental.pallas import tpu as pltpu
from jax.sharding import PartitionSpec as P

HEAD_DIM = 64
F32 = jnp.float32
BF16 = jnp.bfloat16
MOST_PEERS = 8


def swap(block, axis):
    size = lax.axis_size(axis)
    return lax.ppermute(block, axis, [(i, size - 1 - i) for i in range(size)])


def exchange(blocks):
    return lax.all_to_all(blocks, "tok", 0, 0, tiled=False)


def gather(block):
    count = lax.axis_size("tok")
    return exchange(jnp.broadcast_to(block[None], (count,) + block.shape))


def layer_norm(values, eps):
    mean = jnp.mean(values, axis=-1, keepdims=True)
    centred = values - mean
    spread = jnp.mean(centred * centred, axis=-1, keepdims=True)
    return centred * lax.rsqrt(spread + eps)


def three_terms(values):
    high = lax.reduce_precision(values, 8, 7)
    rest = values - high
    middle = lax.reduce_precision(rest, 8, 7)
    return jnp.concatenate([high, middle, rest - middle], axis=-1).astype(BF16)


def from_three(terms):
    terms = terms.astype(F32)
    count = terms.shape[-1] // 3
    return terms[..., :count] + terms[..., count : 2 * count] + terms[..., 2 * count :]


def by_all_to_all(hidden, lengths, text_count, timestep, mod_table, w_qkv, w_out, qk_gain, stale_cache):
    first = lax.axis_index("section") == 0
    own_half = lax.axis_index("section")
    tok_count = lax.axis_size("tok")
    tok_index = lax.axis_index("tok")
    patches, cap_dev, width = hidden.shape
    rows = patches * cap_dev
    total = rows * tok_count
    depth = w_qkv.shape[1]
    half = w_qkv.shape[3] // 2
    heads = half // HEAD_DIM

    def both_layers(own, other):
        return jnp.where(first, own, other), jnp.where(first, other, own)

    def halves(array):
        axis = array.ndim - 1
        keep = lax.dynamic_slice_in_dim(array, own_half * half, half, axis)
        send = lax.dynamic_slice_in_dim(array, (1 - own_half) * half, half, axis)
        return both_layers(keep, swap(send, "section"))

    offsets = jnp.cumsum(lengths) - lengths
    row = jnp.arange(total, dtype=jnp.int32)
    row_patch = (row // cap_dev) % patches
    row_slot = (row // rows) * cap_dev + row % cap_dev
    row_live = row_slot < lengths[row_patch]
    is_text = ((offsets[row_patch] + row_slot) < text_count[0])[:, None]
    own_patch = jnp.arange(rows, dtype=jnp.int32) // cap_dev
    own_live = (tok_index * cap_dev + jnp.arange(rows, dtype=jnp.int32) % cap_dev) < lengths[own_patch]
    cap_all = cap_dev * tok_count
    stale_patch = jnp.arange(patches * cap_all, dtype=jnp.int32) // cap_all
    stale_live = (jnp.arange(patches * cap_all, dtype=jnp.int32) % cap_all) < lengths[stale_patch]
    fresh_seen = row_live[None, :] & (row_patch[None, :] <= own_patch[:, None])
    stale_seen = stale_live[None, :] & (stale_patch[None, :] > own_patch[:, None])
    seen = jnp.concatenate([fresh_seen, stale_seen], axis=1)

    states = hidden.reshape(rows, width).astype(F32)
    mean = jnp.mean(states, axis=-1, keepdims=True)
    centred = states - mean
    inverse = lax.rsqrt(jnp.mean(centred * centred, axis=-1, keepdims=True) + 1e-05)
    stats = three_terms(jnp.concatenate([mean, inverse], axis=-1))
    stats = jnp.pad(stats, ((0, 0), (0, 128 - stats.shape[1])))
    blocks = hidden.reshape(rows, tok_count, depth).transpose(1, 0, 2)
    blocks = jnp.concatenate(
        [blocks, jnp.broadcast_to(stats[None], (tok_count,) + stats.shape)], axis=-1
    )
    arrived = exchange(blocks).reshape(total, depth + 128)
    slices = arrived[:, :depth].astype(F32)
    stats = from_three(arrived[:, depth : depth + 6])

    weight_in = halves(w_qkv[0].transpose(1, 0, 2))
    weight_out = halves(w_out[0])
    stale = halves(stale_cache[0].reshape(2, patches * cap_all, 2 * half))
    modulation = lax.dynamic_index_in_dim(mod_table[0], timestep[0], 0, keepdims=False)
    modulation = lax.dynamic_slice_in_dim(modulation, tok_index * depth, depth, 1)
    modulation = both_layers(modulation, swap(modulation, "section"))
    gains = both_layers(qk_gain[0], swap(qk_gain[0], "section"))

    outputs, caches = [], []
    for layer in range(2):
        if layer:
            part_mean = jnp.mean(slices, axis=-1, keepdims=True)
            off = slices - part_mean
            part = jnp.concatenate([part_mean, jnp.sum(off * off, axis=-1, keepdims=True)], axis=-1)
            parts = gather(part)
            mean = jnp.mean(parts[..., 0], axis=0)
            apart = parts[..., 0] - mean[None]
            spread = jnp.sum(parts[..., 1] + depth * apart * apart, axis=0) / (depth * tok_count)
            stats = jnp.stack([mean, lax.rsqrt(spread + 1e-05)], axis=-1)
        mod = modulation[layer].astype(F32)
        shift = jnp.where(is_text, mod[3], mod[0])
        scale = jnp.where(is_text, mod[4], mod[1])
        gate = jnp.where(is_text, mod[5], mod[2])
        normed = (slices - stats[:, :1]) * stats[:, 1:]
        modded = (normed * (1.0 + scale) + shift).astype(BF16)
        partial = jnp.concatenate(
            [
                jnp.dot(modded, weight_in[layer][i], preferred_element_type=F32).astype(BF16)
                for i in range(3)
            ],
            axis=-1,
        ).reshape(tok_count, rows, 3 * half)
        mixed = jnp.sum(exchange(partial).astype(F32), axis=0).reshape(rows, 3, heads, HEAD_DIM)
        gain = gains[layer]
        queries = (layer_norm(mixed[:, 0], 1e-06) * gain[0]).astype(BF16)
        keys_new = (layer_norm(mixed[:, 1], 1e-06) * gain[1]).astype(BF16)
        fresh = jnp.stack([keys_new, mixed[:, 2].astype(BF16)])
        fresh = jnp.where(own_live[None, :, None, None], fresh, jnp.zeros_like(fresh))
        fresh = gather(fresh.reshape(2, rows, half))
        caches.append(fresh)
        fresh = fresh.transpose(1, 0, 2, 3).reshape(2, total, half)
        keys_values = jnp.concatenate([fresh, stale[layer]], axis=1).reshape(
            2, total + patches * cap_all, heads, HEAD_DIM
        )
        scores = (
            jnp.einsum("qhd,khd->hqk", queries, keys_values[0], preferred_element_type=F32)
            * HEAD_DIM ** (-0.5)
        )
        scores = jnp.where(seen[None], scores, -jnp.inf)
        expo = jnp.exp(scores - jnp.max(scores, axis=-1, keepdims=True))
        weights = (expo / jnp.sum(expo, axis=-1, keepdims=True)).astype(BF16)
        attended = jnp.einsum("hqk,khd->qhd", weights, keys_values[1], preferred_element_type=F32)
        attended = gather(attended.astype(BF16).reshape(rows, half)).reshape(total, half)
        projected = lax.dot_general(
            attended, weight_out[layer], (((1,), (1,)), ((), ())), preferred_element_type=F32
        ).astype(BF16)
        projected = projected.astype(F32) + swap(projected, "section").astype(F32)
        projected = projected.astype(BF16)
        projected = projected.astype(F32) + swap(projected, "fsdp").astype(F32)
        result = jnp.where(row_live[:, None], slices + gate * projected, 0.0).astype(BF16)
        outputs.append(result)
        slices = result.astype(F32)

    final = jnp.where(first, outputs[0], outputs[1]).reshape(tok_count, rows, depth)
    final = exchange(final).transpose(1, 0, 2).reshape(1, patches, cap_dev, width)
    mine = jnp.where(first, caches[0], caches[1])
    theirs = swap(jnp.where(first, caches[1], caches[0]), "section")
    cache = jnp.concatenate(
        [jnp.where(first, mine, theirs), jnp.where(first, theirs, mine)], axis=-1
    ).reshape(tok_count, 2, patches, cap_dev, 2 * half)
    cache = cache.transpose(1, 2, 0, 3, 4).reshape(1, 2, patches, cap_all, 2 * half)
    return final, cache


def iota(shape, dim):
    return lax.broadcasted_iota(jnp.int32, shape, dim)


def total_of(parts):
    total = parts[0]
    for part in parts[1:]:
        total = total + part
    return total


def split_three(value):
    high = value.astype(BF16).astype(F32)
    middle = (value - high).astype(BF16).astype(F32)
    return [high, middle, value - high - middle]


def in_lanes(columns, lanes):
    rows = columns[0].shape[0]
    lane = iota((rows, lanes), 1)
    block = jnp.zeros((rows, lanes), F32)
    for i, column in enumerate(columns):
        block = jnp.where(lane == i, column, block)
    return block.astype(BF16)


def from_columns(block, at):
    return [
        sum(block[:, at + i : at + i + 1] for i in range(3 * j, 3 * j + 3)) for j in range(2)
    ]


def bounds(sizes, patches):
    ends = [sizes[0]]
    for p in range(1, patches):
        ends.append(ends[-1] + sizes[p])
    return ends


def positions(sizes, patch, slot, patches):
    ends = bounds(sizes, patches)
    position = jnp.full(slot.shape, -1, jnp.int32)
    for p in range(patches):
        own = (patch == p) & (slot < sizes[p])
        position = jnp.where(own, slot + (ends[p] - sizes[p]), position)
    return position


def slots_by_device(shape, dim, cap_dev, patches):
    index = iota(shape, dim)
    rows = cap_dev * patches
    return (index // cap_dev) % patches, (index // rows) * cap_dev + index % cap_dev


def slots_by_patch(shape, dim, cap_all):
    index = iota(shape, dim)
    return index // cap_all, index % cap_all


def begin(source, target, sem):
    copy = pltpu.make_async_copy(source, target, sem)
    copy.start()
    return copy


def finish(copies):
    for copy in copies:
        copy.wait()


def send_rows(dims, hidden, out, staged, sems):
    rows = dims.patches * dims.cap_dev
    given = hidden[...].astype(F32).reshape(rows, hidden.shape[2])
    mean = jnp.mean(given, axis=-1, keepdims=True)
    centred = given - mean
    inverse = lax.rsqrt(jnp.mean(centred * centred, axis=-1, keepdims=True) + 1e-05)
    stats = in_lanes(split_three(mean) + split_three(inverse), 128)
    given = given.astype(BF16)
    copies = []
    for i in range(dims.count):
        staged[i, :, : dims.depth] = given[:, i * dims.depth : (i + 1) * dims.depth]
        staged[i, :, dims.depth :] = stats
        copies.append(begin(staged.at[i], out.at[i], sems.at[i]))
    finish(copies)


def modulation_rows(dims, mod, sizes):
    is_text = iota((dims.live, 1), 0) < sizes[dims.patches]
    mod = mod[...].astype(F32)
    return [
        jnp.where(is_text, mod[i + 3 : i + 4, :], mod[i : i + 1, :]) for i in range(3)
    ]


def put_partials(dims, out, staged, sems, query, key, value, extra, stats):
    live, width, groups, turns = dims.live, dims.group_width, dims.groups, dims.turns
    share = live // turns
    fold = share // 2
    sides = key.shape[1] // (groups * width)
    copies = []
    places = [
        (g, h, (h * groups + g % groups) * sides + g // groups)
        for g in range(sides * groups)
        for h in range(turns)
    ]
    for g in range(sides * groups):
        cut = slice(g * width, (g + 1) * width)
        pair = jnp.concatenate([key[:live, cut], value[:live, cut]], axis=1).astype(BF16)
        for other, h, at in places:
            if other == g:
                staged[at, :live, :] = pair
    query = query()
    for g, h, at in places:
        cut = slice(g * width, (g + 1) * width)
        part = query[h * share : (h + 1) * share, cut]
        rows = [jnp.concatenate([part[:fold], part[fold:]], axis=1)]
        if extra:
            last = query[live : live + 4, cut]
            rows += [
                jnp.concatenate([key[live : live + 4, cut], value[live : live + 4, cut]], axis=1),
                jnp.concatenate([last, jnp.zeros_like(last)], axis=1),
            ]
        rows = jnp.concatenate(rows, axis=0)
        staged[at, live : live + rows.shape[0], :] = rows.astype(BF16)
        if extra:
            staged[at, live + fold + 8 :, :] = stats
        copies.append(begin(staged.at[at], out.at[at], sems.at[at]))
    finish(copies)


def own_then_other(dims, wide):
    second = lax.axis_index("tok") % dims.pairs == 1
    left, right = wide[:, : dims.depth], wide[:, dims.depth :]
    return jnp.where(second, right, left), jnp.where(second, left, right)


def load(dims, side, first, weights, out, sems):
    columns = out.shape[2]
    start = pl.multiple_of(lax.axis_index("tok") % dims.pairs * columns, 128) if side else 0
    finish(
        [
            begin(weights.at[first + i, :, pl.ds(start, columns)], out.at[i], sems.at[i])
            for i in range(out.shape[0])
        ]
    )


def first_partials(
    dims, sizes, mod, weights, queries, arrived, kept_states, out, held, sem, staged, sems
):
    copy = begin(queries.at[0], held, sem)
    patch, slot = slots_by_device((1, dims.total), 1, dims.cap_dev, dims.patches)
    position = positions(sizes, patch, slot, dims.patches)
    pick = (iota((dims.live, dims.total), 0) == position).astype(F32).astype(BF16)
    rows = arrived[...].reshape(dims.total, dims.depth + 128)
    states = jnp.dot(pick, rows, preferred_element_type=F32)
    mean, inverse = from_columns(states, dims.depth)
    states = states[:, : dims.depth]
    own_mod = own_then_other(dims, mod[...].astype(F32))[0]
    shift, scale, gate = modulation_rows(dims, own_mod, sizes)
    modded = ((states - mean) * inverse * (1.0 + scale) + shift).astype(BF16)
    kept_states[...] = states.astype(BF16)
    mixed = [jnp.dot(modded, weights[i], preferred_element_type=F32) for i in range(2)]

    def query():
        copy.wait()
        return jnp.dot(modded, held[...], preferred_element_type=F32)

    put_partials(dims, out, staged, sems, query, *mixed, False, None)


def head_means(values, blocks, terms):
    total = None
    for _ in range(terms):
        term = values.astype(BF16)
        part = jnp.dot(term, blocks, preferred_element_type=F32)
        total = part if total is None else total + part
        values = values - term.astype(F32)
    return total * (1.0 / HEAD_DIM)


def head_norm(values, gain, blocks):
    centred = values - head_means(values, blocks, 3)
    spread = head_means(centred * centred, blocks, 2)
    return (centred * lax.rsqrt(spread + 1e-06) * gain).astype(BF16)


def own_share(dims, turn, value, share):
    part = value[:share]
    for h in range(1, dims.turns):
        part = jnp.where(turn == h, value[h * share : (h + 1) * share], part)
    return part


def attention(
    dims, layer, sizes, gains, stale, arrived, attended, cache, fresh_rows, block, sems
):
    count = arrived.shape[0]
    turn = lax.axis_index("tok") // dims.pairs // dims.groups
    live, width = dims.live, dims.group_width
    share = live // dims.turns
    fold = share // 2
    pairs = total_of([arrived[i, :live, :].astype(F32) for i in range(count)])
    height = fold + 8 if layer else fold
    folded = [arrived[i, live : live + height, :].astype(F32) for i in range(count)]
    extras = [part[fold:] for part in folded]
    folded = total_of(folded)
    queries = jnp.concatenate([folded[:fold, :width], folded[:fold, width:]], axis=0)
    if layer:
        is_text = iota((live, 1), 0) < sizes[dims.patches]
        eye = (iota((live, live), 0) == iota((live, live), 1)).astype(F32).astype(BF16)
        means, spreads = [], []
        stats = jnp.concatenate(
            [arrived[i, live + fold + 8 :, :live].astype(F32) for i in range(count)], axis=0
        )
        columns = lax.dot_general(
            eye, stats.astype(BF16), (((1,), (1,)), ((), ())), preferred_element_type=F32
        )
        for i in range(count):
            mean, spread = from_columns(columns, 8 * i)
            means.append(mean)
            spreads.append(spread)
        mean = total_of(means) * (1.0 / count)
        apart = [part - mean for part in means]
        spread = total_of(spreads) + dims.count // count * dims.depth * total_of([part * part for part in apart])
        inverse = lax.rsqrt(spread * (1.0 / (dims.count * dims.depth)) + 1e-05)
        pairs = pairs + total_of(
            [a * jnp.where(is_text, e[0:1], e[1:2]) for a, e in zip(apart, extras)]
        )
        total = total_of(extras)
        pairs = pairs * inverse + jnp.where(is_text, total[2:3], total[3:4])
        mine = functools.partial(own_share, dims, turn, share=share)
        text_mine = (iota((share, 1), 0) + turn * share) < sizes[dims.patches]
        queries = queries + total_of(
            [
                mine(a) * jnp.where(text_mine, e[4:5, :width], e[5:6, :width])
                for a, e in zip(apart, extras)
            ]
        )
        queries = queries * mine(inverse) + jnp.where(text_mine, total[6:7, :width], total[7:8, :width])
    ends = bounds(sizes, dims.patches)
    query_at = iota((share, 1), 0) + turn * share
    query_patch = jnp.zeros((share, 1), jnp.int32)
    for end in ends[:-1]:
        query_patch = query_patch + (query_at >= end).astype(jnp.int32)
    query_end = jnp.zeros((share, 1), jnp.int32)
    for p, end in enumerate(ends):
        query_end = jnp.where(query_patch == p, end, query_end)
    stale_patch, stale_slot = slots_by_patch((1, dims.total), 1, dims.cap_all)
    stale_live = positions(sizes, stale_patch, stale_slot, dims.patches) >= 0
    fresh_seen = iota((share, live), 1) < query_end
    stale_seen = stale_live & (stale_patch > query_patch)
    heads = width // HEAD_DIM
    contract = (((1,), (1,)), ((), ()))
    same = iota((width, width), 0) // HEAD_DIM == iota((width, width), 1) // HEAD_DIM
    blocks = same.astype(F32).astype(BF16)
    gain = [jnp.concatenate([gains[i : i + 1, :]] * heads, axis=1) for i in range(2)]
    query = head_norm(queries, gain[0], blocks).astype(F32)
    key = head_norm(pairs[:, :width], gain[1], blocks)
    value = pairs[:, width:].astype(BF16)
    lanes = iota((heads * share, width), 1) // HEAD_DIM == iota((heads * share, width), 0) // share
    stacked = jnp.where(lanes, jnp.concatenate([query] * heads, axis=0), 0.0).astype(BF16)
    fresh = lax.dot_general(stacked, key, contract, preferred_element_type=F32)
    old = lax.dot_general(stacked, stale[0], contract, preferred_element_type=F32)
    repeated = lambda seen: jnp.concatenate([seen.astype(jnp.int32)] * heads, axis=0) > 0
    fresh = jnp.where(repeated(fresh_seen), fresh * HEAD_DIM ** (-0.5), -jnp.inf)
    old = jnp.where(repeated(stale_seen), old * HEAD_DIM ** (-0.5), -jnp.inf)
    top = jnp.maximum(jnp.max(fresh, axis=-1, keepdims=True), jnp.max(old, axis=-1, keepdims=True))
    fresh, old = jnp.exp(fresh - top), jnp.exp(old - top)
    norm = jnp.sum(fresh, axis=-1, keepdims=True) + jnp.sum(old, axis=-1, keepdims=True)
    fresh, old = (fresh / norm).astype(BF16), (old / norm).astype(BF16)
    outs = jnp.dot(fresh, value, preferred_element_type=F32)
    outs = outs + jnp.dot(old, stale[1], preferred_element_type=F32)
    outs = jnp.where(lanes, outs, 0.0)
    outs = total_of([outs[h * share : (h + 1) * share] for h in range(heads)])
    block[...] = jnp.concatenate([outs[:fold], outs[fold:]], axis=1).astype(BF16)
    copies = [begin(block, attended.at[i], sems.at[i]) for i in range(attended.shape[0])]
    new = jnp.concatenate([key.astype(F32), pairs[:, width:]], axis=1).astype(BF16)
    patch, slot = slots_by_patch((dims.total, 1), 0, dims.cap_all)
    position = positions(sizes, patch, slot, dims.patches)
    spread_out = (iota((dims.total, live), 1) == position).astype(F32).astype(BF16)
    fresh_rows[...] = jnp.dot(spread_out, new, preferred_element_type=F32).astype(BF16)
    copies.append(begin(fresh_rows, cache, sems.at[attended.shape[0]]))
    finish(copies)


def output_rows(dims, sizes, mod, near, states, arrived):
    width = dims.group_width
    rows = []
    for h in range(dims.turns):
        parts = [
            arrived[(h * dims.groups + g) * dims.pairs + y].astype(F32)
            for y in range(dims.pairs)
            for g in range(dims.groups)
        ]
        rows.append(jnp.concatenate([part[:, :width] for part in parts], axis=1))
        rows.append(jnp.concatenate([part[:, width:] for part in parts], axis=1))
    heads = jnp.concatenate(rows, axis=0).astype(BF16)
    projected = lax.dot_general(
        heads, near[...], (((1,), (1,)), ((), ())), preferred_element_type=F32
    )
    gate = own_then_other(dims, modulation_rows(dims, mod, sizes)[2])[0]
    return (from_first(dims, states) + gate * projected).astype(BF16)


def from_first(dims, states):
    half = jnp.zeros((dims.live, 1), jnp.int32) + lax.axis_index("fsdp")
    return jnp.where(half == 0, states.astype(F32), 0.0)


def layer_rows(dims, sizes, mod, near, states, arrived, out):
    out[...] = output_rows(dims, sizes, mod, near, states[...], arrived)


def both(first, second):
    return (first[...].astype(F32) + second[...].astype(F32)).astype(BF16)


def next_partials(
    dims, sizes, mod, weights, swapped, corner, others, across, given, out, staged, sems
):
    states = [both(given, across), both(others, corner)]
    states = jnp.concatenate([part.astype(F32) for part in states], axis=1)
    mean = jnp.mean(states, axis=-1, keepdims=True)
    centred = states - mean
    spread = jnp.sum(centred * centred, axis=-1, keepdims=True)
    stats = in_lanes(split_three(mean) + split_three(spread), 128)
    eye = (iota((dims.live, dims.live), 0) == iota((dims.live, dims.live), 1)).astype(F32).astype(BF16)
    stats = lax.dot_general(stats, eye, (((0,), (0,)), ((), ())), preferred_element_type=F32)[:8]
    lanes = 2 * dims.group_width
    stats = jnp.concatenate([stats, jnp.zeros((8, lanes - dims.live), F32)], axis=1).astype(BF16)
    rows = jnp.concatenate(own_then_other(dims, mod[...].astype(F32)), axis=1)
    is_text = iota((dims.live, 1), 0) < sizes[dims.patches]
    scaled = centred * (1.0 + jnp.where(is_text, rows[4:5], rows[1:2]))
    extra = jnp.concatenate(
        [1.0 + rows[4:5], 1.0 + rows[1:2], rows[3:4], rows[0:1], jnp.zeros_like(rows[:4])], axis=0
    )
    left = jnp.concatenate([scaled, extra], axis=0).astype(BF16)
    mixed = [
        jnp.dot(left[:, : dims.depth], weights[i], preferred_element_type=F32)
        + jnp.dot(left[:, dims.depth :], swapped[i], preferred_element_type=F32)
        for i in range(3)
    ]
    put_partials(dims, out, staged, sems, lambda: mixed[0], *mixed[1:], True, stats)


def last_rows(
    dims, sizes, mod, near, made, back, given, across, first_cache, last_cache, first_side,
    last_side, arrived, out, pair, pieces, staged, sems, fetched, sent
):
    def spread(states):
        patch, slot = slots_by_device((dims.total, 1), 0, dims.cap_dev, dims.patches)
        position = positions(sizes, patch, slot, dims.patches)
        pick = (iota((dims.total, dims.live), 1) == position).astype(F32).astype(BF16)
        blocks = jnp.dot(pick, states, preferred_element_type=F32).astype(BF16)
        staged[...] = blocks.reshape(staged.shape)
        finish(
            [
                begin(staged, out.at[pl.ds(i * dims.count, dims.count)], sems.at[i])
                for i in range(out.shape[0] // dims.count)
            ]
        )

    section = lax.axis_index("section")

    @pl.when(section == 0)
    def _():
        copy = begin(first_cache, pieces.at[0], fetched)
        pieces[1] = first_side[...]
        copy.wait()
        copy = begin(pieces, pair, sent)
        states = from_first(dims, both(made, back)).astype(BF16)
        spread(states)
        copy.wait()

    @pl.when(section != 0)
    def _():
        pieces[0] = last_cache[...]
        pieces[1] = last_side[...]
        copy = begin(pieces, pair, sent)
        states = output_rows(dims, sizes, mod, near, both(given, across), arrived)
        spread(states)
        copy.wait()


def join(dims, arrived, pair, other, out, cache, pieces):
    for i in range(dims.count):
        block = arrived[i].astype(F32) + arrived[dims.count + i].astype(F32)
        block = block.reshape(dims.patches, dims.cap_dev, dims.depth)
        out[0, :, :, i * dims.depth : (i + 1) * dims.depth] = block.astype(BF16)
    groups, width, pairs = dims.groups, dims.group_width, dims.pairs
    own = lax.axis_index("tok")
    line, side = own // pairs, own % pairs
    for g, blocks in enumerate((pair, other)):
        for y in range(pairs):
            pieces[(side ^ y) * groups + (line % groups ^ g)] = blocks[y]
    for i in range(2):
        cut = slice(i * width, (i + 1) * width)
        cache[i] = jnp.concatenate([pieces[j][:, cut] for j in range(groups * pairs)], axis=1)


Dims = collections.namedtuple(
    "Dims",
    [
        "count",
        "pairs",
        "patches",
        "cap_dev",
        "cap_all",
        "total",
        "live",
        "depth",
        "groups",
        "turns",
        "group_width",
    ],
)


class Stays:
    def __init__(self, *shape):
        self.struct = pltpu.VMEM(shape, BF16)


class Leaves:
    def __init__(self, *shape):
        self.struct = pltpu.HBM(shape, BF16)


def only(section, body, *refs):
    @pl.when(lax.axis_index("section") == section)
    def _():
        body(*refs)


def stage(body, outs, smem, *arguments, left=(), scratch=(), grant=16, moved=0):
    spaces = [pltpu.SMEM] * smem + [pltpu.VMEM] * (len(arguments) - smem)
    place = lambda out: pltpu.HBM if isinstance(out, Leaves) else pltpu.VMEM
    out_specs = jax.tree.map(lambda out: pl.BlockSpec(memory_space=place(out)), outs)
    outs = jax.tree.map(lambda out: getattr(out, "struct", out), outs)
    arguments = list(arguments)
    for i in left:
        spaces[i] = pltpu.HBM
        arguments[i] = pltpu.with_memory_space_constraint(arguments[i], pltpu.HBM)
    return pl.pallas_call(
        body,
        out_shape=outs,
        in_specs=[pl.BlockSpec(memory_space=space) for space in spaces],
        out_specs=out_specs,
        scratch_shapes=scratch,
        cost_estimate=pl.CostEstimate(flops=0, bytes_accessed=moved, transcendentals=0) if moved else None,
        compiler_params=pltpu.CompilerParams(vmem_limit_bytes=grant * 1024 * 1024),
    )(*arguments)


def by_kernels(hidden, lengths, text_count, timestep, mod_table, w_qkv, w_out, qk_gain, stale_cache):
    count = lax.axis_size("tok")
    halves = lax.axis_size("fsdp")
    own = lax.axis_index("tok")
    patches, cap_dev, width = hidden.shape
    rows = patches * cap_dev
    total = rows * count
    live = total * 3 // 4
    depth, local_width = w_qkv.shape[1], w_qkv.shape[3]
    pairs = 2
    lines = count // pairs
    line, side = own // pairs, own % pairs
    half_width = local_width // pairs
    groups = math.gcd(half_width // HEAD_DIM, lines)
    turns = lines // groups
    group_width = half_width // groups
    cap_all = cap_dev * count
    dims = Dims(
        count, pairs, patches, cap_dev, cap_all, total, live, depth, groups, turns, group_width
    )
    share = live // turns
    fold = share // 2

    def struct(*shape):
        return jax.ShapeDtypeStruct(shape, BF16)

    kernel = lambda body, *rest: functools.partial(body, dims, *rest)
    working = lambda section, body, *rest: functools.partial(only, section, kernel(body, *rest))
    place = lambda s, f, t: (s * halves + f) * count + t

    def send(block, source, target, df=0, dt=0):
        ends = [
            (place(source, f, t), place(target, f ^ df, t ^ dt))
            for f in range(halves)
            for t in range(count)
        ]
        return lax.ppermute(block, ("section", "fsdp", "tok"), ends)

    def grouped(blocks, section, working, idle):
        sizes = {len(group) for group in working + idle}
        if len(sizes) > 1 or len(working) != len(idle):
            idle = working
        groups = [[place(section, *at) for at in group] for group in working]
        groups += [[place(1 - section, *at) for at in group] for group in idle]
        return lax.all_to_all(
            blocks, ("section", "fsdp", "tok"), 0, 0, axis_index_groups=groups, tiled=False
        )

    def over_tok(blocks, section):
        half = lines // 2
        working = [[(f, t) for t in range(count)] for f in range(halves)]
        idle = [
            [(f, t) for f in range(halves) for t in range(z * pairs, (z + half) * pairs)]
            for z in range(0, lines, half)
        ]
        return grouped(blocks, section, working, idle)

    def over_lines(blocks, section):
        working = [
            [(f, z * pairs + y) for z in range(lines)] for f in range(halves) for y in range(pairs)
        ]
        idle = [
            [(f, z * pairs + y) for f in range(halves) for y in range(pairs)] for z in range(lines)
        ]
        return grouped(blocks, section, working, idle)

    def all_devices(blocks):
        return lax.all_to_all(blocks, ("fsdp", "tok"), 0, 0, tiled=False)

    def after(done, *operands):
        return lax.optimization_barrier((done, *operands))

    height = live + fold
    attended_shape = (
        Leaves(count, fold, 2 * group_width),
        Leaves(total, 2 * group_width),
    )
    kept_rows = (total, 2 * group_width)
    attended_scratch = [
        pltpu.VMEM((fold, 2 * group_width), BF16),
        pltpu.SemaphoreType.DMA((count + 1,)),
    ]
    weights = w_qkv[0].transpose(1, 0, 2)
    near = w_out[0]
    gains = qk_gain[0]
    stale = lax.dynamic_slice_in_dim(
        stale_cache[0].reshape(2, total, local_width),
        side * half_width + line % groups * group_width,
        group_width,
        2,
    )

    blocks = stage(
        kernel(send_rows),
        Leaves(count, rows, depth + 128),
        0,
        hidden,
        scratch=[pltpu.VMEM((count, rows, depth + 128), BF16), pltpu.SemaphoreType.DMA((count,))],
        grant=62,
    )
    blocks, step, lengths, text_count, weights_now = after(
        blocks, timestep, lengths, text_count, weights
    )
    sizes = jnp.concatenate([lengths, text_count])
    loaded_first = stage(
        working(0, load, False, 1),
        Stays(2, depth, local_width),
        0,
        weights_now,
        left=(0,),
        scratch=[pltpu.SemaphoreType.DMA((2,))],
        moved=4 * weights.size,
    )
    arrived = over_tok(blocks, 0)
    mod = lax.dynamic_slice(
        mod_table[0].transpose(1, 0, 2), (0, step[0], line * pairs * depth), (6, 1, pairs * depth)
    )[:, 0]

    states, blocks = stage(
        working(0, first_partials),
        (struct(live, depth), Leaves(count, height, 2 * group_width)),
        1,
        sizes,
        mod,
        loaded_first,
        weights,
        arrived,
        left=(3,),
        scratch=[
            pltpu.VMEM((depth, local_width), BF16),
            pltpu.SemaphoreType.DMA,
            pltpu.VMEM((count, height, 2 * group_width), BF16),
            pltpu.SemaphoreType.DMA((count,)),
        ],
    )
    blocks, weights_now = after(blocks, weights)
    arrived = over_tok(blocks, 0)
    loaded_last = stage(
        working(1, load, True, 0),
        Stays(3, depth, half_width),
        0,
        weights_now,
        left=(0,),
        scratch=[pltpu.SemaphoreType.DMA((3,))],
        moved=4 * weights.size,
    )
    leaving = lax.dynamic_slice_in_dim(weights_now, (1 - side) * half_width, half_width, 2)
    swapped_last = send(leaving, 1, 1, dt=1)
    arrived, swapped_last = after(arrived, swapped_last)

    attended, cache_first = stage(
        working(0, attention, 0),
        attended_shape,
        1,
        sizes,
        gains,
        stale,
        arrived,
        scratch=[pltpu.VMEM(kept_rows, BF16)] + attended_scratch,
    )
    arrived = over_tok(attended, 0)
    made = stage(
        working(0, layer_rows),
        struct(live, depth),
        1,
        sizes,
        mod,
        near,
        states,
        arrived,
    )
    given = send(made, 0, 1)
    across = send(made, 0, 1, df=1)
    others = send(made, 0, 1, dt=1)
    corner = send(made, 0, 1, df=1, dt=1)
    blocks = stage(
        working(1, next_partials),
        Leaves(lines, height + 16, 2 * group_width),
        1,
        sizes,
        mod,
        loaded_last,
        swapped_last,
        corner,
        others,
        across,
        given,
        scratch=[
            pltpu.VMEM((lines, height + 16, 2 * group_width), BF16),
            pltpu.SemaphoreType.DMA((lines,)),
        ],
    )
    blocks, made, cache_first = after(blocks, made, cache_first)
    arrived = over_lines(blocks, 1)
    back = send(made, 0, 0, df=1)
    side_first = send(cache_first, 0, 0, dt=1)
    arrived, back, side_first = after(arrived, back, side_first)

    attended, cache_last, kept_last = stage(
        working(1, attention, 1),
        attended_shape + (Stays(*kept_rows),),
        1,
        sizes,
        gains,
        stale,
        arrived,
        scratch=attended_scratch,
    )
    arrived = over_tok(attended, 1)
    side_last = send(cache_last, 1, 1, dt=1)
    arrived, side_last = after(arrived, side_last)
    blocks, pair, kept_pair = stage(
        kernel(last_rows),
        (
            Leaves(halves * count, rows, depth),
            Leaves(2, total, 2 * group_width),
            Stays(2, total, 2 * group_width),
        ),
        1,
        sizes,
        mod,
        near,
        made,
        back,
        given,
        across,
        cache_first,
        kept_last,
        side_first,
        side_last,
        arrived,
        left=(7,),
        scratch=[
            pltpu.VMEM((count, rows, depth), BF16),
            pltpu.SemaphoreType.DMA((halves,)),
            pltpu.SemaphoreType.DMA,
            pltpu.SemaphoreType.DMA,
        ],
    )
    arrived = all_devices(blocks)
    other = lax.ppermute(pair, "tok", [(t, t ^ pairs) for t in range(count)])
    final, new_cache = stage(
        kernel(join),
        (struct(1, patches, cap_dev, width), struct(2, total, local_width)),
        0,
        arrived,
        kept_pair,
        other,
        scratch=[pltpu.VMEM((groups * pairs, total, 2 * group_width), BF16)],
    )
    return final, new_cache.reshape(1, 2, patches, cap_all, local_width)


def solution(mesh):
    in_specs = (
        P(None, "tok", None),
        P(),
        P(),
        P(),
        P("section", None, None, None),
        P("section", "tok", None, "fsdp"),
        P("section", "tok", "fsdp"),
        P("section", None, None),
        P("section", None, None, None, "fsdp"),
    )
    out_specs = (P("section", None, "tok", None), P("section", None, None, None, "fsdp"))
    local = by_kernels if mesh.shape["tok"] <= MOST_PEERS else by_all_to_all
    return jax.shard_map(local, mesh=mesh, in_specs=in_specs, out_specs=out_specs, check_vma=False)
```

```python
import collections
import functools
import math

import jax
import jax.numpy as jnp
from jax import lax
from jax.experimental import pallas as pl
from jax.experimental.pallas import tpu as pltpu
from jax.sharding import PartitionSpec as P

HEAD_DIM = 64
F32 = jnp.float32
BF16 = jnp.bfloat16
MOST_PEERS = 8


def swap(block, axis):
    size = lax.axis_size(axis)
    return lax.ppermute(block, axis, [(i, size - 1 - i) for i in range(size)])


def exchange(blocks):
    return lax.all_to_all(blocks, "tok", 0, 0, tiled=False)


def gather(block):
    count = lax.axis_size("tok")
    return exchange(jnp.broadcast_to(block[None], (count,) + block.shape))


def layer_norm(values, eps):
    mean = jnp.mean(values, axis=-1, keepdims=True)
    centred = values - mean
    spread = jnp.mean(centred * centred, axis=-1, keepdims=True)
    return centred * lax.rsqrt(spread + eps)


def three_terms(values):
    high = lax.reduce_precision(values, 8, 7)
    rest = values - high
    middle = lax.reduce_precision(rest, 8, 7)
    return jnp.concatenate([high, middle, rest - middle], axis=-1).astype(BF16)


def from_three(terms):
    terms = terms.astype(F32)
    count = terms.shape[-1] // 3
    return terms[..., :count] + terms[..., count : 2 * count] + terms[..., 2 * count :]


def by_all_to_all(hidden, lengths, text_count, timestep, mod_table, w_qkv, w_out, qk_gain, stale_cache):
    first = lax.axis_index("section") == 0
    own_half = lax.axis_index("section")
    tok_count = lax.axis_size("tok")
    tok_index = lax.axis_index("tok")
    patches, cap_dev, width = hidden.shape
    rows = patches * cap_dev
    total = rows * tok_count
    depth = w_qkv.shape[1]
    half = w_qkv.shape[3] // 2
    heads = half // HEAD_DIM

    def both_layers(own, other):
        return jnp.where(first, own, other), jnp.where(first, other, own)

    def halves(array):
        axis = array.ndim - 1
        keep = lax.dynamic_slice_in_dim(array, own_half * half, half, axis)
        send = lax.dynamic_slice_in_dim(array, (1 - own_half) * half, half, axis)
        return both_layers(keep, swap(send, "section"))

    offsets = jnp.cumsum(lengths) - lengths
    row = jnp.arange(total, dtype=jnp.int32)
    row_patch = (row // cap_dev) % patches
    row_slot = (row // rows) * cap_dev + row % cap_dev
    row_live = row_slot < lengths[row_patch]
    is_text = ((offsets[row_patch] + row_slot) < text_count[0])[:, None]
    own_patch = jnp.arange(rows, dtype=jnp.int32) // cap_dev
    own_live = (tok_index * cap_dev + jnp.arange(rows, dtype=jnp.int32) % cap_dev) < lengths[own_patch]
    cap_all = cap_dev * tok_count
    stale_patch = jnp.arange(patches * cap_all, dtype=jnp.int32) // cap_all
    stale_live = (jnp.arange(patches * cap_all, dtype=jnp.int32) % cap_all) < lengths[stale_patch]
    fresh_seen = row_live[None, :] & (row_patch[None, :] <= own_patch[:, None])
    stale_seen = stale_live[None, :] & (stale_patch[None, :] > own_patch[:, None])
    seen = jnp.concatenate([fresh_seen, stale_seen], axis=1)

    states = hidden.reshape(rows, width).astype(F32)
    mean = jnp.mean(states, axis=-1, keepdims=True)
    centred = states - mean
    inverse = lax.rsqrt(jnp.mean(centred * centred, axis=-1, keepdims=True) + 1e-05)
    stats = three_terms(jnp.concatenate([mean, inverse], axis=-1))
    stats = jnp.pad(stats, ((0, 0), (0, 128 - stats.shape[1])))
    blocks = hidden.reshape(rows, tok_count, depth).transpose(1, 0, 2)
    blocks = jnp.concatenate(
        [blocks, jnp.broadcast_to(stats[None], (tok_count,) + stats.shape)], axis=-1
    )
    arrived = exchange(blocks).reshape(total, depth + 128)
    slices = arrived[:, :depth].astype(F32)
    stats = from_three(arrived[:, depth : depth + 6])

    weight_in = halves(w_qkv[0].transpose(1, 0, 2))
    weight_out = halves(w_out[0])
    stale = halves(stale_cache[0].reshape(2, patches * cap_all, 2 * half))
    modulation = lax.dynamic_index_in_dim(mod_table[0], timestep[0], 0, keepdims=False)
    modulation = lax.dynamic_slice_in_dim(modulation, tok_index * depth, depth, 1)
    modulation = both_layers(modulation, swap(modulation, "section"))
    gains = both_layers(qk_gain[0], swap(qk_gain[0], "section"))

    outputs, caches = [], []
    for layer in range(2):
        if layer:
            part_mean = jnp.mean(slices, axis=-1, keepdims=True)
            off = slices - part_mean
            part = jnp.concatenate([part_mean, jnp.sum(off * off, axis=-1, keepdims=True)], axis=-1)
            parts = gather(part)
            mean = jnp.mean(parts[..., 0], axis=0)
            apart = parts[..., 0] - mean[None]
            spread = jnp.sum(parts[..., 1] + depth * apart * apart, axis=0) / (depth * tok_count)
            stats = jnp.stack([mean, lax.rsqrt(spread + 1e-05)], axis=-1)
        mod = modulation[layer].astype(F32)
        shift = jnp.where(is_text, mod[3], mod[0])
        scale = jnp.where(is_text, mod[4], mod[1])
        gate = jnp.where(is_text, mod[5], mod[2])
        normed = (slices - stats[:, :1]) * stats[:, 1:]
        modded = (normed * (1.0 + scale) + shift).astype(BF16)
        partial = jnp.concatenate(
            [
                jnp.dot(modded, weight_in[layer][i], preferred_element_type=F32).astype(BF16)
                for i in range(3)
            ],
            axis=-1,
        ).reshape(tok_count, rows, 3 * half)
        mixed = jnp.sum(exchange(partial).astype(F32), axis=0).reshape(rows, 3, heads, HEAD_DIM)
        gain = gains[layer]
        queries = (layer_norm(mixed[:, 0], 1e-06) * gain[0]).astype(BF16)
        keys_new = (layer_norm(mixed[:, 1], 1e-06) * gain[1]).astype(BF16)
        fresh = jnp.stack([keys_new, mixed[:, 2].astype(BF16)])
        fresh = jnp.where(own_live[None, :, None, None], fresh, jnp.zeros_like(fresh))
        fresh = gather(fresh.reshape(2, rows, half))
        caches.append(fresh)
        fresh = fresh.transpose(1, 0, 2, 3).reshape(2, total, half)
        keys_values = jnp.concatenate([fresh, stale[layer]], axis=1).reshape(
            2, total + patches * cap_all, heads, HEAD_DIM
        )
        scores = (
            jnp.einsum("qhd,khd->hqk", queries, keys_values[0], preferred_element_type=F32)
            * HEAD_DIM ** (-0.5)
        )
        scores = jnp.where(seen[None], scores, -jnp.inf)
        expo = jnp.exp(scores - jnp.max(scores, axis=-1, keepdims=True))
        weights = (expo / jnp.sum(expo, axis=-1, keepdims=True)).astype(BF16)
        attended = jnp.einsum("hqk,khd->qhd", weights, keys_values[1], preferred_element_type=F32)
        attended = gather(attended.astype(BF16).reshape(rows, half)).reshape(total, half)
        projected = lax.dot_general(
            attended, weight_out[layer], (((1,), (1,)), ((), ())), preferred_element_type=F32
        ).astype(BF16)
        projected = projected.astype(F32) + swap(projected, "section").astype(F32)
        projected = projected.astype(BF16)
        projected = projected.astype(F32) + swap(projected, "fsdp").astype(F32)
        result = jnp.where(row_live[:, None], slices + gate * projected, 0.0).astype(BF16)
        outputs.append(result)
        slices = result.astype(F32)

    final = jnp.where(first, outputs[0], outputs[1]).reshape(tok_count, rows, depth)
    final = exchange(final).transpose(1, 0, 2).reshape(1, patches, cap_dev, width)
    mine = jnp.where(first, caches[0], caches[1])
    theirs = swap(jnp.where(first, caches[1], caches[0]), "section")
    cache = jnp.concatenate(
        [jnp.where(first, mine, theirs), jnp.where(first, theirs, mine)], axis=-1
    ).reshape(tok_count, 2, patches, cap_dev, 2 * half)
    cache = cache.transpose(1, 2, 0, 3, 4).reshape(1, 2, patches, cap_all, 2 * half)
    return final, cache


def iota(shape, dim):
    return lax.broadcasted_iota(jnp.int32, shape, dim)


def total_of(parts):
    total = parts[0]
    for part in parts[1:]:
        total = total + part
    return total


def split_three(value):
    high = value.astype(BF16).astype(F32)
    middle = (value - high).astype(BF16).astype(F32)
    return [high, middle, value - high - middle]


def in_lanes(columns, lanes):
    rows = columns[0].shape[0]
    lane = iota((rows, lanes), 1)
    block = jnp.zeros((rows, lanes), F32)
    for i, column in enumerate(columns):
        block = jnp.where(lane == i, column, block)
    return block.astype(BF16)


def from_columns(block, at):
    return [
        sum(block[:, at + i : at + i + 1] for i in range(3 * j, 3 * j + 3)) for j in range(2)
    ]


def bounds(sizes, patches):
    ends = [sizes[0]]
    for p in range(1, patches):
        ends.append(ends[-1] + sizes[p])
    return ends


def positions(sizes, patch, slot, patches):
    ends = bounds(sizes, patches)
    position = jnp.full(slot.shape, -1, jnp.int32)
    for p in range(patches):
        own = (patch == p) & (slot < sizes[p])
        position = jnp.where(own, slot + (ends[p] - sizes[p]), position)
    return position


def slots_by_device(shape, dim, cap_dev, patches):
    index = iota(shape, dim)
    rows = cap_dev * patches
    return (index // cap_dev) % patches, (index // rows) * cap_dev + index % cap_dev


def slots_by_patch(shape, dim, cap_all):
    index = iota(shape, dim)
    return index // cap_all, index % cap_all


def begin(source, target, sem):
    copy = pltpu.make_async_copy(source, target, sem)
    copy.start()
    return copy


def finish(copies):
    for copy in copies:
        copy.wait()


def send_rows(dims, hidden, out, staged, sems):
    rows = dims.patches * dims.cap_dev
    given = hidden[...].astype(F32).reshape(rows, hidden.shape[2])
    mean = jnp.mean(given, axis=-1, keepdims=True)
    centred = given - mean
    inverse = lax.rsqrt(jnp.mean(centred * centred, axis=-1, keepdims=True) + 1e-05)
    stats = in_lanes(split_three(mean) + split_three(inverse), 128)
    given = given.astype(BF16)
    copies = []
    for i in range(dims.count):
        staged[i, :, : dims.depth] = given[:, i * dims.depth : (i + 1) * dims.depth]
        staged[i, :, dims.depth :] = stats
        copies.append(begin(staged.at[i], out.at[i], sems.at[i]))
    finish(copies)


def modulation_rows(dims, mod, sizes):
    is_text = iota((dims.live, 1), 0) < sizes[dims.patches]
    mod = mod[...].astype(F32)
    return [
        jnp.where(is_text, mod[i + 3 : i + 4, :], mod[i : i + 1, :]) for i in range(3)
    ]


def put_partials(dims, out, staged, sems, query, key, value, extra, stats):
    live, width, groups, turns = dims.live, dims.group_width, dims.groups, dims.turns
    share = live // turns
    fold = share // 2
    sides = key.shape[1] // (groups * width)
    copies = []
    places = [
        (g, h, (h * groups + g % groups) * sides + g // groups)
        for g in range(sides * groups)
        for h in range(turns)
    ]
    for g in range(sides * groups):
        cut = slice(g * width, (g + 1) * width)
        pair = jnp.concatenate([key[:live, cut], value[:live, cut]], axis=1).astype(BF16)
        for other, h, at in places:
            if other == g:
                staged[at, :live, :] = pair
    query = query()
    for g, h, at in places:
        cut = slice(g * width, (g + 1) * width)
        part = query[h * share : (h + 1) * share, cut]
        rows = [jnp.concatenate([part[:fold], part[fold:]], axis=1)]
        if extra:
            last = query[live : live + 4, cut]
            rows += [
                jnp.concatenate([key[live : live + 4, cut], value[live : live + 4, cut]], axis=1),
                jnp.concatenate([last, jnp.zeros_like(last)], axis=1),
            ]
        rows = jnp.concatenate(rows, axis=0)
        staged[at, live : live + rows.shape[0], :] = rows.astype(BF16)
        if extra:
            staged[at, live + fold + 8 :, :] = stats
        copies.append(begin(staged.at[at], out.at[at], sems.at[at]))
    finish(copies)


def own_then_other(dims, wide):
    second = lax.axis_index("tok") % dims.pairs == 1
    left, right = wide[:, : dims.depth], wide[:, dims.depth :]
    return jnp.where(second, right, left), jnp.where(second, left, right)


def load(dims, side, first, weights, out, sems):
    columns = out.shape[2]
    start = pl.multiple_of(lax.axis_index("tok") % dims.pairs * columns, 128) if side else 0
    finish(
        [
            begin(weights.at[first + i, :, pl.ds(start, columns)], out.at[i], sems.at[i])
            for i in range(out.shape[0])
        ]
    )


def first_partials(
    dims, sizes, mod, weights, queries, arrived, kept_states, out, held, sem, staged, sems
):
    copy = begin(queries.at[0], held, sem)
    patch, slot = slots_by_device((1, dims.total), 1, dims.cap_dev, dims.patches)
    position = positions(sizes, patch, slot, dims.patches)
    pick = (iota((dims.live, dims.total), 0) == position).astype(F32).astype(BF16)
    rows = arrived[...].reshape(dims.total, dims.depth + 128)
    states = jnp.dot(pick, rows, preferred_element_type=F32)
    mean, inverse = from_columns(states, dims.depth)
    states = states[:, : dims.depth]
    own_mod = own_then_other(dims, mod[...].astype(F32))[0]
    shift, scale, gate = modulation_rows(dims, own_mod, sizes)
    modded = ((states - mean) * inverse * (1.0 + scale) + shift).astype(BF16)
    kept_states[...] = states.astype(BF16)
    mixed = [jnp.dot(modded, weights[i], preferred_element_type=F32) for i in range(2)]

    def query():
        copy.wait()
        return jnp.dot(modded, held[...], preferred_element_type=F32)

    put_partials(dims, out, staged, sems, query, *mixed, False, None)


def head_means(values, blocks, terms):
    total = None
    for _ in range(terms):
        term = values.astype(BF16)
        part = jnp.dot(term, blocks, preferred_element_type=F32)
        total = part if total is None else total + part
        values = values - term.astype(F32)
    return total * (1.0 / HEAD_DIM)


def head_norm(values, gain, blocks):
    centred = values - head_means(values, blocks, 3)
    spread = head_means(centred * centred, blocks, 2)
    return (centred * lax.rsqrt(spread + 1e-06) * gain).astype(BF16)


def own_share(dims, turn, value, share):
    part = value[:share]
    for h in range(1, dims.turns):
        part = jnp.where(turn == h, value[h * share : (h + 1) * share], part)
    return part


def attention(
    dims, layer, sizes, gains, stale, arrived, attended, cache, fresh_rows, block, sems
):
    count = arrived.shape[0]
    turn = lax.axis_index("tok") // dims.pairs // dims.groups
    live, width = dims.live, dims.group_width
    share = live // dims.turns
    fold = share // 2
    pairs = total_of([arrived[i, :live, :].astype(F32) for i in range(count)])
    height = fold + 8 if layer else fold
    folded = [arrived[i, live : live + height, :].astype(F32) for i in range(count)]
    extras = [part[fold:] for part in folded]
    folded = total_of(folded)
    queries = jnp.concatenate([folded[:fold, :width], folded[:fold, width:]], axis=0)
    if layer:
        is_text = iota((live, 1), 0) < sizes[dims.patches]
        eye = (iota((live, live), 0) == iota((live, live), 1)).astype(F32).astype(BF16)
        means, spreads = [], []
        stats = jnp.concatenate(
            [arrived[i, live + fold + 8 :, :live].astype(F32) for i in range(count)], axis=0
        )
        columns = lax.dot_general(
            eye, stats.astype(BF16), (((1,), (1,)), ((), ())), preferred_element_type=F32
        )
        for i in range(count):
            mean, spread = from_columns(columns, 8 * i)
            means.append(mean)
            spreads.append(spread)
        mean = total_of(means) * (1.0 / count)
        apart = [part - mean for part in means]
        spread = total_of(spreads) + dims.count // count * dims.depth * total_of([part * part for part in apart])
        inverse = lax.rsqrt(spread * (1.0 / (dims.count * dims.depth)) + 1e-05)
        pairs = pairs + total_of(
            [a * jnp.where(is_text, e[0:1], e[1:2]) for a, e in zip(apart, extras)]
        )
        total = total_of(extras)
        pairs = pairs * inverse + jnp.where(is_text, total[2:3], total[3:4])
        mine = functools.partial(own_share, dims, turn, share=share)
        text_mine = (iota((share, 1), 0) + turn * share) < sizes[dims.patches]
        queries = queries + total_of(
            [
                mine(a) * jnp.where(text_mine, e[4:5, :width], e[5:6, :width])
                for a, e in zip(apart, extras)
            ]
        )
        queries = queries * mine(inverse) + jnp.where(text_mine, total[6:7, :width], total[7:8, :width])
    ends = bounds(sizes, dims.patches)
    query_at = iota((share, 1), 0) + turn * share
    query_patch = jnp.zeros((share, 1), jnp.int32)
    for end in ends[:-1]:
        query_patch = query_patch + (query_at >= end).astype(jnp.int32)
    query_end = jnp.zeros((share, 1), jnp.int32)
    for p, end in enumerate(ends):
        query_end = jnp.where(query_patch == p, end, query_end)
    stale_patch, stale_slot = slots_by_patch((1, dims.total), 1, dims.cap_all)
    stale_live = positions(sizes, stale_patch, stale_slot, dims.patches) >= 0
    fresh_seen = iota((share, live), 1) < query_end
    stale_seen = stale_live & (stale_patch > query_patch)
    heads = width // HEAD_DIM
    contract = (((1,), (1,)), ((), ()))
    same = iota((width, width), 0) // HEAD_DIM == iota((width, width), 1) // HEAD_DIM
    blocks = same.astype(F32).astype(BF16)
    gain = [jnp.concatenate([gains[i : i + 1, :]] * heads, axis=1) for i in range(2)]
    query = head_norm(queries, gain[0], blocks).astype(F32)
    key = head_norm(pairs[:, :width], gain[1], blocks)
    value = pairs[:, width:].astype(BF16)
    lanes = iota((heads * share, width), 1) // HEAD_DIM == iota((heads * share, width), 0) // share
    stacked = jnp.where(lanes, jnp.concatenate([query] * heads, axis=0), 0.0).astype(BF16)
    fresh = lax.dot_general(stacked, key, contract, preferred_element_type=F32)
    old = lax.dot_general(stacked, stale[0], contract, preferred_element_type=F32)
    repeated = lambda seen: jnp.concatenate([seen.astype(jnp.int32)] * heads, axis=0) > 0
    fresh = jnp.where(repeated(fresh_seen), fresh * HEAD_DIM ** (-0.5), -jnp.inf)
    old = jnp.where(repeated(stale_seen), old * HEAD_DIM ** (-0.5), -jnp.inf)
    top = jnp.maximum(jnp.max(fresh, axis=-1, keepdims=True), jnp.max(old, axis=-1, keepdims=True))
    fresh, old = jnp.exp(fresh - top), jnp.exp(old - top)
    norm = jnp.sum(fresh, axis=-1, keepdims=True) + jnp.sum(old, axis=-1, keepdims=True)
    fresh, old = (fresh / norm).astype(BF16), (old / norm).astype(BF16)
    outs = jnp.dot(fresh, value, preferred_element_type=F32)
    outs = outs + jnp.dot(old, stale[1], preferred_element_type=F32)
    outs = jnp.where(lanes, outs, 0.0)
    outs = total_of([outs[h * share : (h + 1) * share] for h in range(heads)])
    block[...] = jnp.concatenate([outs[:fold], outs[fold:]], axis=1).astype(BF16)
    copies = [begin(block, attended.at[i], sems.at[i]) for i in range(attended.shape[0])]
    new = jnp.concatenate([key.astype(F32), pairs[:, width:]], axis=1).astype(BF16)
    patch, slot = slots_by_patch((dims.total, 1), 0, dims.cap_all)
    position = positions(sizes, patch, slot, dims.patches)
    spread_out = (iota((dims.total, live), 1) == position).astype(F32).astype(BF16)
    fresh_rows[...] = jnp.dot(spread_out, new, preferred_element_type=F32).astype(BF16)
    copies.append(begin(fresh_rows, cache, sems.at[attended.shape[0]]))
    finish(copies)


def output_rows(dims, sizes, mod, near, states, arrived):
    width = dims.group_width
    rows = []
    for h in range(dims.turns):
        parts = [
            arrived[(h * dims.groups + g) * dims.pairs + y].astype(F32)
            for y in range(dims.pairs)
            for g in range(dims.groups)
        ]
        rows.append(jnp.concatenate([part[:, :width] for part in parts], axis=1))
        rows.append(jnp.concatenate([part[:, width:] for part in parts], axis=1))
    heads = jnp.concatenate(rows, axis=0).astype(BF16)
    projected = lax.dot_general(
        heads, near[...], (((1,), (1,)), ((), ())), preferred_element_type=F32
    )
    gate = own_then_other(dims, modulation_rows(dims, mod, sizes)[2])[0]
    return (from_first(dims, states) + gate * projected).astype(BF16)


def from_first(dims, states):
    half = jnp.zeros((dims.live, 1), jnp.int32) + lax.axis_index("fsdp")
    return jnp.where(half == 0, states.astype(F32), 0.0)


def layer_rows(dims, sizes, mod, near, states, arrived, out):
    out[...] = output_rows(dims, sizes, mod, near, states[...], arrived)


def both(first, second):
    return (first[...].astype(F32) + second[...].astype(F32)).astype(BF16)


def next_partials(
    dims, sizes, mod, weights, swapped, corner, others, across, given, out, staged, sems
):
    states = [both(given, across), both(others, corner)]
    states = jnp.concatenate([part.astype(F32) for part in states], axis=1)
    mean = jnp.mean(states, axis=-1, keepdims=True)
    centred = states - mean
    spread = jnp.sum(centred * centred, axis=-1, keepdims=True)
    stats = in_lanes(split_three(mean) + split_three(spread), 128)
    eye = (iota((dims.live, dims.live), 0) == iota((dims.live, dims.live), 1)).astype(F32).astype(BF16)
    stats = lax.dot_general(stats, eye, (((0,), (0,)), ((), ())), preferred_element_type=F32)[:8]
    lanes = 2 * dims.group_width
    stats = jnp.concatenate([stats, jnp.zeros((8, lanes - dims.live), F32)], axis=1).astype(BF16)
    rows = jnp.concatenate(own_then_other(dims, mod[...].astype(F32)), axis=1)
    is_text = iota((dims.live, 1), 0) < sizes[dims.patches]
    scaled = centred * (1.0 + jnp.where(is_text, rows[4:5], rows[1:2]))
    extra = jnp.concatenate(
        [1.0 + rows[4:5], 1.0 + rows[1:2], rows[3:4], rows[0:1], jnp.zeros_like(rows[:4])], axis=0
    )
    left = jnp.concatenate([scaled, extra], axis=0).astype(BF16)
    mixed = [
        jnp.dot(left[:, : dims.depth], weights[i], preferred_element_type=F32)
        + jnp.dot(left[:, dims.depth :], swapped[i], preferred_element_type=F32)
        for i in range(3)
    ]
    put_partials(dims, out, staged, sems, lambda: mixed[0], *mixed[1:], True, stats)


def last_rows(
    dims, sizes, mod, near, made, given, across, first_cache, last_cache, first_side,
    last_side, arrived, out, pair, pieces, staged, sems, fetched, sent
):
    def spread(states):
        patch, slot = slots_by_device((dims.total, 1), 0, dims.cap_dev, dims.patches)
        position = positions(sizes, patch, slot, dims.patches)
        pick = (iota((dims.total, dims.live), 1) == position).astype(F32).astype(BF16)
        blocks = jnp.dot(pick, states, preferred_element_type=F32).astype(BF16)
        staged[...] = blocks.reshape(staged.shape)
        finish(
            [
                begin(staged, out.at[pl.ds(i * dims.count, dims.count)], sems.at[i])
                for i in range(out.shape[0] // dims.count)
            ]
        )

    section = lax.axis_index("section")

    @pl.when(section == 0)
    def _():
        copy = begin(first_cache, pieces.at[0], fetched)
        pieces[1] = first_side[...]
        copy.wait()
        copy = begin(pieces, pair, sent)
        states = made[...]
        spread(states)
        copy.wait()

    @pl.when(section != 0)
    def _():
        pieces[0] = last_cache[...]
        pieces[1] = last_side[...]
        copy = begin(pieces, pair, sent)
        states = output_rows(dims, sizes, mod, near, both(given, across), arrived)
        spread(states)
        copy.wait()


def join(dims, arrived, pair, other, out, cache, pieces):
    for i in range(dims.count):
        block = arrived[i].astype(F32) + arrived[dims.count + i].astype(F32)
        block = block.reshape(dims.patches, dims.cap_dev, dims.depth)
        out[0, :, :, i * dims.depth : (i + 1) * dims.depth] = block.astype(BF16)
    groups, width, pairs = dims.groups, dims.group_width, dims.pairs
    own = lax.axis_index("tok")
    line, side = own // pairs, own % pairs
    for g, blocks in enumerate((pair, other)):
        for y in range(pairs):
            pieces[(side ^ y) * groups + (line % groups ^ g)] = blocks[y]
    for i in range(2):
        cut = slice(i * width, (i + 1) * width)
        cache[i] = jnp.concatenate([pieces[j][:, cut] for j in range(groups * pairs)], axis=1)


Dims = collections.namedtuple(
    "Dims",
    [
        "count",
        "pairs",
        "patches",
        "cap_dev",
        "cap_all",
        "total",
        "live",
        "depth",
        "groups",
        "turns",
        "group_width",
    ],
)


class Stays:
    def __init__(self, *shape):
        self.struct = pltpu.VMEM(shape, BF16)


class Leaves:
    def __init__(self, *shape):
        self.struct = pltpu.HBM(shape, BF16)


def only(section, body, *refs):
    @pl.when(lax.axis_index("section") == section)
    def _():
        body(*refs)


def stage(body, outs, smem, *arguments, left=(), scratch=(), grant=16, moved=0):
    spaces = [pltpu.SMEM] * smem + [pltpu.VMEM] * (len(arguments) - smem)
    place = lambda out: pltpu.HBM if isinstance(out, Leaves) else pltpu.VMEM
    out_specs = jax.tree.map(lambda out: pl.BlockSpec(memory_space=place(out)), outs)
    outs = jax.tree.map(lambda out: getattr(out, "struct", out), outs)
    arguments = list(arguments)
    for i in left:
        spaces[i] = pltpu.HBM
        arguments[i] = pltpu.with_memory_space_constraint(arguments[i], pltpu.HBM)
    return pl.pallas_call(
        body,
        out_shape=outs,
        in_specs=[pl.BlockSpec(memory_space=space) for space in spaces],
        out_specs=out_specs,
        scratch_shapes=scratch,
        cost_estimate=pl.CostEstimate(flops=0, bytes_accessed=moved, transcendentals=0) if moved else None,
        compiler_params=pltpu.CompilerParams(vmem_limit_bytes=grant * 1024 * 1024),
    )(*arguments)


def by_kernels(hidden, lengths, text_count, timestep, mod_table, w_qkv, w_out, qk_gain, stale_cache):
    count = lax.axis_size("tok")
    halves = lax.axis_size("fsdp")
    own = lax.axis_index("tok")
    patches, cap_dev, width = hidden.shape
    rows = patches * cap_dev
    total = rows * count
    live = total * 3 // 4
    depth, local_width = w_qkv.shape[1], w_qkv.shape[3]
    pairs = 2
    lines = count // pairs
    line, side = own // pairs, own % pairs
    half_width = local_width // pairs
    groups = math.gcd(half_width // HEAD_DIM, lines)
    turns = lines // groups
    group_width = half_width // groups
    cap_all = cap_dev * count
    dims = Dims(
        count, pairs, patches, cap_dev, cap_all, total, live, depth, groups, turns, group_width
    )
    share = live // turns
    fold = share // 2

    def struct(*shape):
        return jax.ShapeDtypeStruct(shape, BF16)

    kernel = lambda body, *rest: functools.partial(body, dims, *rest)
    working = lambda section, body, *rest: functools.partial(only, section, kernel(body, *rest))
    place = lambda s, f, t: (s * halves + f) * count + t

    def send(block, source, target, df=0, dt=0):
        ends = [
            (place(source, f, t), place(target, f ^ df, t ^ dt))
            for f in range(halves)
            for t in range(count)
        ]
        return lax.ppermute(block, ("section", "fsdp", "tok"), ends)

    def grouped(blocks, section, working, idle):
        sizes = {len(group) for group in working + idle}
        if len(sizes) > 1 or len(working) != len(idle):
            idle = working
        groups = [[place(section, *at) for at in group] for group in working]
        groups += [[place(1 - section, *at) for at in group] for group in idle]
        return lax.all_to_all(
            blocks, ("section", "fsdp", "tok"), 0, 0, axis_index_groups=groups, tiled=False
        )

    def over_tok(blocks, section):
        half = lines // 2
        working = [[(f, t) for t in range(count)] for f in range(halves)]
        idle = [
            [(f, t) for f in range(halves) for t in range(z * pairs, (z + half) * pairs)]
            for z in range(0, lines, half)
        ]
        return grouped(blocks, section, working, idle)

    def over_lines(blocks, section):
        working = [
            [(f, z * pairs + y) for z in range(lines)] for f in range(halves) for y in range(pairs)
        ]
        idle = [
            [(f, z * pairs + y) for f in range(halves) for y in range(pairs)] for z in range(lines)
        ]
        return grouped(blocks, section, working, idle)

    def all_devices(blocks):
        return lax.all_to_all(blocks, ("fsdp", "tok"), 0, 0, tiled=False)

    def after(done, *operands):
        return lax.optimization_barrier((done, *operands))

    height = live + fold
    attended_shape = (
        Leaves(count, fold, 2 * group_width),
        Leaves(total, 2 * group_width),
    )
    kept_rows = (total, 2 * group_width)
    attended_scratch = [
        pltpu.VMEM((fold, 2 * group_width), BF16),
        pltpu.SemaphoreType.DMA((count + 1,)),
    ]
    weights = w_qkv[0].transpose(1, 0, 2)
    near = w_out[0]
    gains = qk_gain[0]
    stale = lax.dynamic_slice_in_dim(
        stale_cache[0].reshape(2, total, local_width),
        side * half_width + line % groups * group_width,
        group_width,
        2,
    )

    blocks = stage(
        kernel(send_rows),
        Leaves(count, rows, depth + 128),
        0,
        hidden,
        scratch=[pltpu.VMEM((count, rows, depth + 128), BF16), pltpu.SemaphoreType.DMA((count,))],
        grant=62,
    )
    blocks, step, lengths, text_count, weights_now = after(
        blocks, timestep, lengths, text_count, weights
    )
    sizes = jnp.concatenate([lengths, text_count])
    loaded_first = stage(
        working(0, load, False, 1),
        Stays(2, depth, local_width),
        0,
        weights_now,
        left=(0,),
        scratch=[pltpu.SemaphoreType.DMA((2,))],
        moved=4 * weights.size,
    )
    arrived = over_tok(blocks, 0)
    mod = lax.dynamic_slice(
        mod_table[0].transpose(1, 0, 2), (0, step[0], line * pairs * depth), (6, 1, pairs * depth)
    )[:, 0]

    states, blocks = stage(
        working(0, first_partials),
        (struct(live, depth), Leaves(count, height, 2 * group_width)),
        1,
        sizes,
        mod,
        loaded_first,
        weights,
        arrived,
        left=(3,),
        scratch=[
            pltpu.VMEM((depth, local_width), BF16),
            pltpu.SemaphoreType.DMA,
            pltpu.VMEM((count, height, 2 * group_width), BF16),
            pltpu.SemaphoreType.DMA((count,)),
        ],
    )
    blocks, weights_now = after(blocks, weights)
    arrived = over_tok(blocks, 0)
    loaded_last = stage(
        working(1, load, True, 0),
        Stays(3, depth, half_width),
        0,
        weights_now,
        left=(0,),
        scratch=[pltpu.SemaphoreType.DMA((3,))],
        moved=4 * weights.size,
    )
    leaving = lax.dynamic_slice_in_dim(weights_now, (1 - side) * half_width, half_width, 2)
    swapped_last = send(leaving, 1, 1, dt=1)
    arrived, swapped_last = after(arrived, swapped_last)

    attended, cache_first = stage(
        working(0, attention, 0),
        attended_shape,
        1,
        sizes,
        gains,
        stale,
        arrived,
        scratch=[pltpu.VMEM(kept_rows, BF16)] + attended_scratch,
    )
    arrived = over_tok(attended, 0)
    made = stage(
        working(0, layer_rows),
        struct(live, depth),
        1,
        sizes,
        mod,
        near,
        states,
        arrived,
    )
    given = send(made, 0, 1)
    across = send(made, 0, 1, df=1)
    others = send(made, 0, 1, dt=1)
    corner = send(made, 0, 1, df=1, dt=1)
    blocks = stage(
        working(1, next_partials),
        Leaves(lines, height + 16, 2 * group_width),
        1,
        sizes,
        mod,
        loaded_last,
        swapped_last,
        corner,
        others,
        across,
        given,
        scratch=[
            pltpu.VMEM((lines, height + 16, 2 * group_width), BF16),
            pltpu.SemaphoreType.DMA((lines,)),
        ],
    )
    blocks, cache_first = after(blocks, cache_first)
    arrived = over_lines(blocks, 1)
    side_first = send(cache_first, 0, 0, dt=1)
    arrived, side_first = after(arrived, side_first)

    attended, cache_last, kept_last = stage(
        working(1, attention, 1),
        attended_shape + (Stays(*kept_rows),),
        1,
        sizes,
        gains,
        stale,
        arrived,
        scratch=attended_scratch,
    )
    arrived = over_tok(attended, 1)
    side_last = send(cache_last, 1, 1, dt=1)
    arrived, side_last = after(arrived, side_last)
    blocks, pair, kept_pair = stage(
        kernel(last_rows),
        (
            Leaves(halves * count, rows, depth),
            Leaves(2, total, 2 * group_width),
            Stays(2, total, 2 * group_width),
        ),
        1,
        sizes,
        mod,
        near,
        made,
        given,
        across,
        cache_first,
        kept_last,
        side_first,
        side_last,
        arrived,
        left=(6,),
        scratch=[
            pltpu.VMEM((count, rows, depth), BF16),
            pltpu.SemaphoreType.DMA((halves,)),
            pltpu.SemaphoreType.DMA,
            pltpu.SemaphoreType.DMA,
        ],
    )
    arrived = all_devices(blocks)
    other = lax.ppermute(pair, "tok", [(t, t ^ pairs) for t in range(count)])
    final, new_cache = stage(
        kernel(join),
        (struct(1, patches, cap_dev, width), struct(2, total, local_width)),
        0,
        arrived,
        kept_pair,
        other,
        scratch=[pltpu.VMEM((groups * pairs, total, 2 * group_width), BF16)],
    )
    return final, new_cache.reshape(1, 2, patches, cap_all, local_width)


def solution(mesh):
    in_specs = (
        P(None, "tok", None),
        P(),
        P(),
        P(),
        P("section", None, None, None),
        P("section", "tok", None, "fsdp"),
        P("section", "tok", "fsdp"),
        P("section", None, None),
        P("section", None, None, None, "fsdp"),
    )
    out_specs = (P("section", None, "tok", None), P("section", None, None, None, "fsdp"))
    local = by_kernels if mesh.shape["tok"] <= MOST_PEERS else by_all_to_all
    return jax.shard_map(local, mesh=mesh, in_specs=in_specs, out_specs=out_specs, check_vma=False)
```

```python
import collections
import functools
import math

import jax
import jax.numpy as jnp
from jax import lax
from jax.experimental import pallas as pl
from jax.experimental.pallas import tpu as pltpu
from jax.sharding import PartitionSpec as P

HEAD_DIM = 64
F32 = jnp.float32
BF16 = jnp.bfloat16
MOST_PEERS = 8


def swap(block, axis):
    size = lax.axis_size(axis)
    return lax.ppermute(block, axis, [(i, size - 1 - i) for i in range(size)])


def exchange(blocks):
    return lax.all_to_all(blocks, "tok", 0, 0, tiled=False)


def gather(block):
    count = lax.axis_size("tok")
    return exchange(jnp.broadcast_to(block[None], (count,) + block.shape))


def layer_norm(values, eps):
    mean = jnp.mean(values, axis=-1, keepdims=True)
    centred = values - mean
    spread = jnp.mean(centred * centred, axis=-1, keepdims=True)
    return centred * lax.rsqrt(spread + eps)


def three_terms(values):
    high = lax.reduce_precision(values, 8, 7)
    rest = values - high
    middle = lax.reduce_precision(rest, 8, 7)
    return jnp.concatenate([high, middle, rest - middle], axis=-1).astype(BF16)


def from_three(terms):
    terms = terms.astype(F32)
    count = terms.shape[-1] // 3
    return terms[..., :count] + terms[..., count : 2 * count] + terms[..., 2 * count :]


def by_all_to_all(hidden, lengths, text_count, timestep, mod_table, w_qkv, w_out, qk_gain, stale_cache):
    first = lax.axis_index("section") == 0
    own_half = lax.axis_index("section")
    tok_count = lax.axis_size("tok")
    tok_index = lax.axis_index("tok")
    patches, cap_dev, width = hidden.shape
    rows = patches * cap_dev
    total = rows * tok_count
    depth = w_qkv.shape[1]
    half = w_qkv.shape[3] // 2
    heads = half // HEAD_DIM

    def both_layers(own, other):
        return jnp.where(first, own, other), jnp.where(first, other, own)

    def halves(array):
        axis = array.ndim - 1
        keep = lax.dynamic_slice_in_dim(array, own_half * half, half, axis)
        send = lax.dynamic_slice_in_dim(array, (1 - own_half) * half, half, axis)
        return both_layers(keep, swap(send, "section"))

    offsets = jnp.cumsum(lengths) - lengths
    row = jnp.arange(total, dtype=jnp.int32)
    row_patch = (row // cap_dev) % patches
    row_slot = (row // rows) * cap_dev + row % cap_dev
    row_live = row_slot < lengths[row_patch]
    is_text = ((offsets[row_patch] + row_slot) < text_count[0])[:, None]
    own_patch = jnp.arange(rows, dtype=jnp.int32) // cap_dev
    own_live = (tok_index * cap_dev + jnp.arange(rows, dtype=jnp.int32) % cap_dev) < lengths[own_patch]
    cap_all = cap_dev * tok_count
    stale_patch = jnp.arange(patches * cap_all, dtype=jnp.int32) // cap_all
    stale_live = (jnp.arange(patches * cap_all, dtype=jnp.int32) % cap_all) < lengths[stale_patch]
    fresh_seen = row_live[None, :] & (row_patch[None, :] <= own_patch[:, None])
    stale_seen = stale_live[None, :] & (stale_patch[None, :] > own_patch[:, None])
    seen = jnp.concatenate([fresh_seen, stale_seen], axis=1)

    states = hidden.reshape(rows, width).astype(F32)
    mean = jnp.mean(states, axis=-1, keepdims=True)
    centred = states - mean
    inverse = lax.rsqrt(jnp.mean(centred * centred, axis=-1, keepdims=True) + 1e-05)
    stats = three_terms(jnp.concatenate([mean, inverse], axis=-1))
    stats = jnp.pad(stats, ((0, 0), (0, 128 - stats.shape[1])))
    blocks = hidden.reshape(rows, tok_count, depth).transpose(1, 0, 2)
    blocks = jnp.concatenate(
        [blocks, jnp.broadcast_to(stats[None], (tok_count,) + stats.shape)], axis=-1
    )
    arrived = exchange(blocks).reshape(total, depth + 128)
    slices = arrived[:, :depth].astype(F32)
    stats = from_three(arrived[:, depth : depth + 6])

    weight_in = halves(w_qkv[0].transpose(1, 0, 2))
    weight_out = halves(w_out[0])
    stale = halves(stale_cache[0].reshape(2, patches * cap_all, 2 * half))
    modulation = lax.dynamic_index_in_dim(mod_table[0], timestep[0], 0, keepdims=False)
    modulation = lax.dynamic_slice_in_dim(modulation, tok_index * depth, depth, 1)
    modulation = both_layers(modulation, swap(modulation, "section"))
    gains = both_layers(qk_gain[0], swap(qk_gain[0], "section"))

    outputs, caches = [], []
    for layer in range(2):
        if layer:
            part_mean = jnp.mean(slices, axis=-1, keepdims=True)
            off = slices - part_mean
            part = jnp.concatenate([part_mean, jnp.sum(off * off, axis=-1, keepdims=True)], axis=-1)
            parts = gather(part)
            mean = jnp.mean(parts[..., 0], axis=0)
            apart = parts[..., 0] - mean[None]
            spread = jnp.sum(parts[..., 1] + depth * apart * apart, axis=0) / (depth * tok_count)
            stats = jnp.stack([mean, lax.rsqrt(spread + 1e-05)], axis=-1)
        mod = modulation[layer].astype(F32)
        shift = jnp.where(is_text, mod[3], mod[0])
        scale = jnp.where(is_text, mod[4], mod[1])
        gate = jnp.where(is_text, mod[5], mod[2])
        normed = (slices - stats[:, :1]) * stats[:, 1:]
        modded = (normed * (1.0 + scale) + shift).astype(BF16)
        partial = jnp.concatenate(
            [
                jnp.dot(modded, weight_in[layer][i], preferred_element_type=F32).astype(BF16)
                for i in range(3)
            ],
            axis=-1,
        ).reshape(tok_count, rows, 3 * half)
        mixed = jnp.sum(exchange(partial).astype(F32), axis=0).reshape(rows, 3, heads, HEAD_DIM)
        gain = gains[layer]
        queries = (layer_norm(mixed[:, 0], 1e-06) * gain[0]).astype(BF16)
        keys_new = (layer_norm(mixed[:, 1], 1e-06) * gain[1]).astype(BF16)
        fresh = jnp.stack([keys_new, mixed[:, 2].astype(BF16)])
        fresh = jnp.where(own_live[None, :, None, None], fresh, jnp.zeros_like(fresh))
        fresh = gather(fresh.reshape(2, rows, half))
        caches.append(fresh)
        fresh = fresh.transpose(1, 0, 2, 3).reshape(2, total, half)
        keys_values = jnp.concatenate([fresh, stale[layer]], axis=1).reshape(
            2, total + patches * cap_all, heads, HEAD_DIM
        )
        scores = (
            jnp.einsum("qhd,khd->hqk", queries, keys_values[0], preferred_element_type=F32)
            * HEAD_DIM ** (-0.5)
        )
        scores = jnp.where(seen[None], scores, -jnp.inf)
        expo = jnp.exp(scores - jnp.max(scores, axis=-1, keepdims=True))
        weights = (expo / jnp.sum(expo, axis=-1, keepdims=True)).astype(BF16)
        attended = jnp.einsum("hqk,khd->qhd", weights, keys_values[1], preferred_element_type=F32)
        attended = gather(attended.astype(BF16).reshape(rows, half)).reshape(total, half)
        projected = lax.dot_general(
            attended, weight_out[layer], (((1,), (1,)), ((), ())), preferred_element_type=F32
        ).astype(BF16)
        projected = projected.astype(F32) + swap(projected, "section").astype(F32)
        projected = projected.astype(BF16)
        projected = projected.astype(F32) + swap(projected, "fsdp").astype(F32)
        result = jnp.where(row_live[:, None], slices + gate * projected, 0.0).astype(BF16)
        outputs.append(result)
        slices = result.astype(F32)

    final = jnp.where(first, outputs[0], outputs[1]).reshape(tok_count, rows, depth)
    final = exchange(final).transpose(1, 0, 2).reshape(1, patches, cap_dev, width)
    mine = jnp.where(first, caches[0], caches[1])
    theirs = swap(jnp.where(first, caches[1], caches[0]), "section")
    cache = jnp.concatenate(
        [jnp.where(first, mine, theirs), jnp.where(first, theirs, mine)], axis=-1
    ).reshape(tok_count, 2, patches, cap_dev, 2 * half)
    cache = cache.transpose(1, 2, 0, 3, 4).reshape(1, 2, patches, cap_all, 2 * half)
    return final, cache


def iota(shape, dim):
    return lax.broadcasted_iota(jnp.int32, shape, dim)


def total_of(parts):
    total = parts[0]
    for part in parts[1:]:
        total = total + part
    return total


def split_three(value):
    high = value.astype(BF16).astype(F32)
    middle = (value - high).astype(BF16).astype(F32)
    return [high, middle, value - high - middle]


def in_lanes(columns, lanes):
    rows = columns[0].shape[0]
    lane = iota((rows, lanes), 1)
    block = jnp.zeros((rows, lanes), F32)
    for i, column in enumerate(columns):
        block = jnp.where(lane == i, column, block)
    return block.astype(BF16)


def from_columns(block, at):
    return [
        sum(block[:, at + i : at + i + 1] for i in range(3 * j, 3 * j + 3)) for j in range(2)
    ]


def bounds(sizes, patches):
    ends = [sizes[0]]
    for p in range(1, patches):
        ends.append(ends[-1] + sizes[p])
    return ends


def positions(sizes, patch, slot, patches):
    ends = bounds(sizes, patches)
    position = jnp.full(slot.shape, -1, jnp.int32)
    for p in range(patches):
        own = (patch == p) & (slot < sizes[p])
        position = jnp.where(own, slot + (ends[p] - sizes[p]), position)
    return position


def slots_by_device(shape, dim, cap_dev, patches):
    index = iota(shape, dim)
    rows = cap_dev * patches
    return (index // cap_dev) % patches, (index // rows) * cap_dev + index % cap_dev


def slots_by_patch(shape, dim, cap_all):
    index = iota(shape, dim)
    return index // cap_all, index % cap_all


def begin(source, target, sem):
    copy = pltpu.make_async_copy(source, target, sem)
    copy.start()
    return copy


def finish(copies):
    for copy in copies:
        copy.wait()


def send_rows(dims, hidden, out, staged, sems):
    rows = dims.patches * dims.cap_dev
    given = hidden[...].astype(F32).reshape(rows, hidden.shape[2])
    mean = jnp.mean(given, axis=-1, keepdims=True)
    centred = given - mean
    inverse = lax.rsqrt(jnp.mean(centred * centred, axis=-1, keepdims=True) + 1e-05)
    stats = in_lanes(split_three(mean) + split_three(inverse), 128)
    given = given.astype(BF16)
    copies = []
    for i in range(dims.count):
        staged[i, :, : dims.depth] = given[:, i * dims.depth : (i + 1) * dims.depth]
        staged[i, :, dims.depth :] = stats
        copies.append(begin(staged.at[i], out.at[i], sems.at[i]))
    finish(copies)


def modulation_rows(dims, mod, sizes):
    is_text = iota((dims.live, 1), 0) < sizes[dims.patches]
    mod = mod[...].astype(F32)
    return [
        jnp.where(is_text, mod[i + 3 : i + 4, :], mod[i : i + 1, :]) for i in range(3)
    ]


def put_partials(dims, out, staged, sems, query, key, value, extra, stats):
    live, width, groups, turns = dims.live, dims.group_width, dims.groups, dims.turns
    share = live // turns
    fold = share // 2
    sides = key.shape[1] // (groups * width)
    copies = []
    places = [
        (g, h, (h * groups + g % groups) * sides + g // groups)
        for g in range(sides * groups)
        for h in range(turns)
    ]
    for g in range(sides * groups):
        cut = slice(g * width, (g + 1) * width)
        pair = jnp.concatenate([key[:live, cut], value[:live, cut]], axis=1).astype(BF16)
        for other, h, at in places:
            if other == g:
                staged[at, :live, :] = pair
    query = query()
    for g, h, at in places:
        cut = slice(g * width, (g + 1) * width)
        part = query[h * share : (h + 1) * share, cut]
        rows = [jnp.concatenate([part[:fold], part[fold:]], axis=1)]
        if extra:
            last = query[live : live + 4, cut]
            rows += [
                jnp.concatenate([key[live : live + 4, cut], value[live : live + 4, cut]], axis=1),
                jnp.concatenate([last, jnp.zeros_like(last)], axis=1),
            ]
        rows = jnp.concatenate(rows, axis=0)
        staged[at, live : live + rows.shape[0], :] = rows.astype(BF16)
        if extra:
            staged[at, live + fold + 8 :, :] = stats
        copies.append(begin(staged.at[at], out.at[at], sems.at[at]))
    finish(copies)


def own_then_other(dims, wide):
    second = lax.axis_index("tok") % dims.pairs == 1
    left, right = wide[:, : dims.depth], wide[:, dims.depth :]
    return jnp.where(second, right, left), jnp.where(second, left, right)


def load(dims, side, first, weights, out, sems):
    columns = out.shape[2]
    start = pl.multiple_of(lax.axis_index("tok") % dims.pairs * columns, 128) if side else 0
    finish(
        [
            begin(weights.at[first + i, :, pl.ds(start, columns)], out.at[i], sems.at[i])
            for i in range(out.shape[0])
        ]
    )


def first_partials(
    dims, sizes, mod, weights, queries, arrived, kept_states, out, held, sem, staged, sems
):
    copy = begin(queries.at[0], held, sem)
    patch, slot = slots_by_device((1, dims.total), 1, dims.cap_dev, dims.patches)
    position = positions(sizes, patch, slot, dims.patches)
    pick = (iota((dims.live, dims.total), 0) == position).astype(F32).astype(BF16)
    rows = arrived[...].reshape(dims.total, dims.depth + 128)
    states = jnp.dot(pick, rows, preferred_element_type=F32)
    mean, inverse = from_columns(states, dims.depth)
    states = states[:, : dims.depth]
    own_mod = own_then_other(dims, mod[...].astype(F32))[0]
    shift, scale, gate = modulation_rows(dims, own_mod, sizes)
    modded = ((states - mean) * inverse * (1.0 + scale) + shift).astype(BF16)
    kept_states[...] = states.astype(BF16)
    mixed = [jnp.dot(modded, weights[i], preferred_element_type=F32) for i in range(2)]

    def query():
        copy.wait()
        return jnp.dot(modded, held[...], preferred_element_type=F32)

    put_partials(dims, out, staged, sems, query, *mixed, False, None)


def head_means(values, blocks, terms):
    total = None
    for _ in range(terms):
        term = values.astype(BF16)
        part = jnp.dot(term, blocks, preferred_element_type=F32)
        total = part if total is None else total + part
        values = values - term.astype(F32)
    return total * (1.0 / HEAD_DIM)


def head_norm(values, gain, blocks):
    centred = values - head_means(values, blocks, 3)
    spread = head_means(centred * centred, blocks, 2)
    return (centred * lax.rsqrt(spread + 1e-06) * gain).astype(BF16)


def own_share(dims, turn, value, share):
    part = value[:share]
    for h in range(1, dims.turns):
        part = jnp.where(turn == h, value[h * share : (h + 1) * share], part)
    return part


def attention(
    dims, layer, sizes, gains, stale, arrived, attended, cache, fresh_rows, block, sems
):
    count = arrived.shape[0]
    turn = lax.axis_index("tok") // dims.pairs // dims.groups
    live, width = dims.live, dims.group_width
    share = live // dims.turns
    fold = share // 2
    pairs = total_of([arrived[i, :live, :].astype(F32) for i in range(count)])
    height = fold + 8 if layer else fold
    folded = [arrived[i, live : live + height, :].astype(F32) for i in range(count)]
    extras = [part[fold:] for part in folded]
    folded = total_of(folded)
    queries = jnp.concatenate([folded[:fold, :width], folded[:fold, width:]], axis=0)
    if layer:
        is_text = iota((live, 1), 0) < sizes[dims.patches]
        eye = (iota((live, live), 0) == iota((live, live), 1)).astype(F32).astype(BF16)
        means, spreads = [], []
        stats = jnp.concatenate(
            [arrived[i, live + fold + 8 :, :live].astype(F32) for i in range(count)], axis=0
        )
        columns = lax.dot_general(
            eye, stats.astype(BF16), (((1,), (1,)), ((), ())), preferred_element_type=F32
        )
        for i in range(count):
            mean, spread = from_columns(columns, 8 * i)
            means.append(mean)
            spreads.append(spread)
        mean = total_of(means) * (1.0 / count)
        apart = [part - mean for part in means]
        spread = total_of(spreads) + dims.count // count * dims.depth * total_of([part * part for part in apart])
        inverse = lax.rsqrt(spread * (1.0 / (dims.count * dims.depth)) + 1e-05)
        pairs = pairs + total_of(
            [a * jnp.where(is_text, e[0:1], e[1:2]) for a, e in zip(apart, extras)]
        )
        total = total_of(extras)
        pairs = pairs * inverse + jnp.where(is_text, total[2:3], total[3:4])
        mine = functools.partial(own_share, dims, turn, share=share)
        text_mine = (iota((share, 1), 0) + turn * share) < sizes[dims.patches]
        queries = queries + total_of(
            [
                mine(a) * jnp.where(text_mine, e[4:5, :width], e[5:6, :width])
                for a, e in zip(apart, extras)
            ]
        )
        queries = queries * mine(inverse) + jnp.where(text_mine, total[6:7, :width], total[7:8, :width])
    ends = bounds(sizes, dims.patches)
    query_at = iota((share, 1), 0) + turn * share
    query_patch = jnp.zeros((share, 1), jnp.int32)
    for end in ends[:-1]:
        query_patch = query_patch + (query_at >= end).astype(jnp.int32)
    query_end = jnp.zeros((share, 1), jnp.int32)
    for p, end in enumerate(ends):
        query_end = jnp.where(query_patch == p, end, query_end)
    stale_patch, stale_slot = slots_by_patch((1, dims.total), 1, dims.cap_all)
    stale_live = positions(sizes, stale_patch, stale_slot, dims.patches) >= 0
    fresh_seen = iota((share, live), 1) < query_end
    stale_seen = stale_live & (stale_patch > query_patch)
    heads = width // HEAD_DIM
    contract = (((1,), (1,)), ((), ()))
    same = iota((width, width), 0) // HEAD_DIM == iota((width, width), 1) // HEAD_DIM
    blocks = same.astype(F32).astype(BF16)
    gain = [jnp.concatenate([gains[i : i + 1, :]] * heads, axis=1) for i in range(2)]
    query = head_norm(queries, gain[0], blocks).astype(F32)
    key = head_norm(pairs[:, :width], gain[1], blocks)
    value = pairs[:, width:].astype(BF16)
    lanes = iota((heads * share, width), 1) // HEAD_DIM == iota((heads * share, width), 0) // share
    stacked = jnp.where(lanes, jnp.concatenate([query] * heads, axis=0), 0.0).astype(BF16)
    fresh = lax.dot_general(stacked, key, contract, preferred_element_type=F32)
    old = lax.dot_general(stacked, stale[0], contract, preferred_element_type=F32)
    repeated = lambda seen: jnp.concatenate([seen.astype(jnp.int32)] * heads, axis=0) > 0
    fresh = jnp.where(repeated(fresh_seen), fresh * HEAD_DIM ** (-0.5), -jnp.inf)
    old = jnp.where(repeated(stale_seen), old * HEAD_DIM ** (-0.5), -jnp.inf)
    top = jnp.maximum(jnp.max(fresh, axis=-1, keepdims=True), jnp.max(old, axis=-1, keepdims=True))
    fresh, old = jnp.exp(fresh - top), jnp.exp(old - top)
    norm = jnp.sum(fresh, axis=-1, keepdims=True) + jnp.sum(old, axis=-1, keepdims=True)
    fresh, old = (fresh / norm).astype(BF16), (old / norm).astype(BF16)
    outs = jnp.dot(fresh, value, preferred_element_type=F32)
    outs = outs + jnp.dot(old, stale[1], preferred_element_type=F32)
    outs = jnp.where(lanes, outs, 0.0)
    outs = total_of([outs[h * share : (h + 1) * share] for h in range(heads)])
    block[...] = jnp.concatenate([outs[:fold], outs[fold:]], axis=1).astype(BF16)
    copies = [begin(block, attended.at[i], sems.at[i]) for i in range(attended.shape[0])]
    new = jnp.concatenate([key.astype(F32), pairs[:, width:]], axis=1).astype(BF16)
    patch, slot = slots_by_patch((dims.total, 1), 0, dims.cap_all)
    position = positions(sizes, patch, slot, dims.patches)
    spread_out = (iota((dims.total, live), 1) == position).astype(F32).astype(BF16)
    fresh_rows[...] = jnp.dot(spread_out, new, preferred_element_type=F32).astype(BF16)
    copies.append(begin(fresh_rows, cache, sems.at[attended.shape[0]]))
    finish(copies)


def output_rows(dims, sizes, mod, near, states, arrived):
    width = dims.group_width
    rows = []
    for h in range(dims.turns):
        parts = [
            arrived[(h * dims.groups + g) * dims.pairs + y].astype(F32)
            for y in range(dims.pairs)
            for g in range(dims.groups)
        ]
        rows.append(jnp.concatenate([part[:, :width] for part in parts], axis=1))
        rows.append(jnp.concatenate([part[:, width:] for part in parts], axis=1))
    heads = jnp.concatenate(rows, axis=0).astype(BF16)
    projected = lax.dot_general(
        heads, near[...], (((1,), (1,)), ((), ())), preferred_element_type=F32
    )
    gate = own_then_other(dims, modulation_rows(dims, mod, sizes)[2])[0]
    return (from_first(dims, states) + gate * projected).astype(BF16)


def from_first(dims, states):
    half = jnp.zeros((dims.live, 1), jnp.int32) + lax.axis_index("fsdp")
    return jnp.where(half == 0, states.astype(F32), 0.0)


def layer_rows(dims, sizes, mod, near, states, arrived, out):
    out[...] = output_rows(dims, sizes, mod, near, states[...], arrived)


def both(first, second):
    return (first[...].astype(F32) + second[...].astype(F32)).astype(BF16)


def next_partials(
    dims, sizes, mod, weights, swapped, corner, others, across, given, out, staged, sems
):
    states = [both(given, across), both(others, corner)]
    states = jnp.concatenate([part.astype(F32) for part in states], axis=1)
    mean = jnp.mean(states, axis=-1, keepdims=True)
    centred = states - mean
    spread = jnp.sum(centred * centred, axis=-1, keepdims=True)
    stats = in_lanes(split_three(mean) + split_three(spread), 128)
    eye = (iota((dims.live, dims.live), 0) == iota((dims.live, dims.live), 1)).astype(F32).astype(BF16)
    stats = lax.dot_general(stats, eye, (((0,), (0,)), ((), ())), preferred_element_type=F32)[:8]
    lanes = 2 * dims.group_width
    stats = jnp.concatenate([stats, jnp.zeros((8, lanes - dims.live), F32)], axis=1).astype(BF16)
    rows = jnp.concatenate(own_then_other(dims, mod[...].astype(F32)), axis=1)
    is_text = iota((dims.live, 1), 0) < sizes[dims.patches]
    scaled = centred * (1.0 + jnp.where(is_text, rows[4:5], rows[1:2]))
    extra = jnp.concatenate(
        [1.0 + rows[4:5], 1.0 + rows[1:2], rows[3:4], rows[0:1], jnp.zeros_like(rows[:4])], axis=0
    )
    left = jnp.concatenate([scaled, extra], axis=0).astype(BF16)
    mixed = [
        jnp.dot(left[:, : dims.depth], weights[i], preferred_element_type=F32)
        + jnp.dot(left[:, dims.depth :], swapped[i], preferred_element_type=F32)
        for i in range(3)
    ]
    put_partials(dims, out, staged, sems, lambda: mixed[0], *mixed[1:], True, stats)


def last_rows(
    dims, sizes, mod, near, made, first_cache, last_cache, first_side, last_side, given, across,
    arrived, out, pair, pieces, staged, sems, fetched, sent
):
    def spread(states):
        patch, slot = slots_by_device((dims.total, 1), 0, dims.cap_dev, dims.patches)
        position = positions(sizes, patch, slot, dims.patches)
        pick = (iota((dims.total, dims.live), 1) == position).astype(F32).astype(BF16)
        blocks = jnp.dot(pick, states, preferred_element_type=F32).astype(BF16)
        staged[...] = blocks.reshape(staged.shape)
        finish(
            [
                begin(staged, out.at[pl.ds(i * dims.count, dims.count)], sems.at[i])
                for i in range(out.shape[0] // dims.count)
            ]
        )

    section = lax.axis_index("section")

    @pl.when(section == 0)
    def _():
        copy = begin(first_cache, pieces.at[0], fetched)
        pieces[1] = first_side[...]
        copy.wait()
        copy = begin(pieces, pair, sent)
        states = made[...]
        spread(states)
        copy.wait()

    @pl.when(section != 0)
    def _():
        pieces[0] = last_cache[...]
        pieces[1] = last_side[...]
        copy = begin(pieces, pair, sent)
        states = output_rows(dims, sizes, mod, near, both(given, across), arrived)
        spread(states)
        copy.wait()


def join(dims, arrived, pair, other, out, cache, pieces):
    for i in range(dims.count):
        block = arrived[i].astype(F32) + arrived[dims.count + i].astype(F32)
        block = block.reshape(dims.patches, dims.cap_dev, dims.depth)
        out[0, :, :, i * dims.depth : (i + 1) * dims.depth] = block.astype(BF16)
    groups, width, pairs = dims.groups, dims.group_width, dims.pairs
    own = lax.axis_index("tok")
    line, side = own // pairs, own % pairs
    for g, blocks in enumerate((pair, other)):
        for y in range(pairs):
            pieces[(side ^ y) * groups + (line % groups ^ g)] = blocks[y]
    for i in range(2):
        cut = slice(i * width, (i + 1) * width)
        cache[i] = jnp.concatenate([pieces[j][:, cut] for j in range(groups * pairs)], axis=1)


Dims = collections.namedtuple(
    "Dims",
    [
        "count",
        "pairs",
        "patches",
        "cap_dev",
        "cap_all",
        "total",
        "live",
        "depth",
        "groups",
        "turns",
        "group_width",
    ],
)


class Stays:
    def __init__(self, *shape):
        self.struct = pltpu.VMEM(shape, BF16)


class Leaves:
    def __init__(self, *shape):
        self.struct = pltpu.HBM(shape, BF16)


def only(section, body, *refs):
    @pl.when(lax.axis_index("section") == section)
    def _():
        body(*refs)


def stage(body, outs, smem, *arguments, left=(), scratch=(), grant=16, moved=0):
    spaces = [pltpu.SMEM] * smem + [pltpu.VMEM] * (len(arguments) - smem)
    place = lambda out: pltpu.HBM if isinstance(out, Leaves) else pltpu.VMEM
    out_specs = jax.tree.map(lambda out: pl.BlockSpec(memory_space=place(out)), outs)
    outs = jax.tree.map(lambda out: getattr(out, "struct", out), outs)
    arguments = list(arguments)
    for i in left:
        spaces[i] = pltpu.HBM
        arguments[i] = pltpu.with_memory_space_constraint(arguments[i], pltpu.HBM)
    return pl.pallas_call(
        body,
        out_shape=outs,
        in_specs=[pl.BlockSpec(memory_space=space) for space in spaces],
        out_specs=out_specs,
        scratch_shapes=scratch,
        cost_estimate=pl.CostEstimate(flops=0, bytes_accessed=moved, transcendentals=0) if moved else None,
        compiler_params=pltpu.CompilerParams(vmem_limit_bytes=grant * 1024 * 1024),
    )(*arguments)


def by_kernels(hidden, lengths, text_count, timestep, mod_table, w_qkv, w_out, qk_gain, stale_cache):
    count = lax.axis_size("tok")
    halves = lax.axis_size("fsdp")
    own = lax.axis_index("tok")
    patches, cap_dev, width = hidden.shape
    rows = patches * cap_dev
    total = rows * count
    live = total * 3 // 4
    depth, local_width = w_qkv.shape[1], w_qkv.shape[3]
    pairs = 2
    lines = count // pairs
    line, side = own // pairs, own % pairs
    half_width = local_width // pairs
    groups = math.gcd(half_width // HEAD_DIM, lines)
    turns = lines // groups
    group_width = half_width // groups
    cap_all = cap_dev * count
    dims = Dims(
        count, pairs, patches, cap_dev, cap_all, total, live, depth, groups, turns, group_width
    )
    share = live // turns
    fold = share // 2

    def struct(*shape):
        return jax.ShapeDtypeStruct(shape, BF16)

    kernel = lambda body, *rest: functools.partial(body, dims, *rest)
    working = lambda section, body, *rest: functools.partial(only, section, kernel(body, *rest))
    place = lambda s, f, t: (s * halves + f) * count + t

    def send(block, source, target, df=0, dt=0):
        ends = [
            (place(source, f, t), place(target, f ^ df, t ^ dt))
            for f in range(halves)
            for t in range(count)
        ]
        return lax.ppermute(block, ("section", "fsdp", "tok"), ends)

    def grouped(blocks, section, working, idle):
        sizes = {len(group) for group in working + idle}
        if len(sizes) > 1 or len(working) != len(idle):
            idle = working
        groups = [[place(section, *at) for at in group] for group in working]
        groups += [[place(1 - section, *at) for at in group] for group in idle]
        return lax.all_to_all(
            blocks, ("section", "fsdp", "tok"), 0, 0, axis_index_groups=groups, tiled=False
        )

    def over_tok(blocks, section):
        half = lines // 2
        working = [[(f, t) for t in range(count)] for f in range(halves)]
        idle = [
            [(f, t) for f in range(halves) for t in range(z * pairs, (z + half) * pairs)]
            for z in range(0, lines, half)
        ]
        return grouped(blocks, section, working, idle)

    def over_lines(blocks, section):
        working = [
            [(f, z * pairs + y) for z in range(lines)] for f in range(halves) for y in range(pairs)
        ]
        idle = [
            [(f, z * pairs + y) for f in range(halves) for y in range(pairs)] for z in range(lines)
        ]
        return grouped(blocks, section, working, idle)

    def all_devices(blocks):
        return lax.all_to_all(blocks, ("fsdp", "tok"), 0, 0, tiled=False)

    def after(done, *operands):
        return lax.optimization_barrier((done, *operands))

    height = live + fold
    attended_shape = (
        Leaves(count, fold, 2 * group_width),
        Leaves(total, 2 * group_width),
    )
    kept_rows = (total, 2 * group_width)
    attended_scratch = [
        pltpu.VMEM((fold, 2 * group_width), BF16),
        pltpu.SemaphoreType.DMA((count + 1,)),
    ]
    weights = w_qkv[0].transpose(1, 0, 2)
    near = w_out[0]
    gains = qk_gain[0]
    stale = lax.dynamic_slice_in_dim(
        stale_cache[0].reshape(2, total, local_width),
        side * half_width + line % groups * group_width,
        group_width,
        2,
    )

    blocks = stage(
        kernel(send_rows),
        Leaves(count, rows, depth + 128),
        0,
        hidden,
        scratch=[pltpu.VMEM((count, rows, depth + 128), BF16), pltpu.SemaphoreType.DMA((count,))],
        grant=62,
    )
    blocks, step, lengths, text_count, weights_now = after(
        blocks, timestep, lengths, text_count, weights
    )
    sizes = jnp.concatenate([lengths, text_count])
    loaded_first = stage(
        working(0, load, False, 1),
        Stays(2, depth, local_width),
        0,
        weights_now,
        left=(0,),
        scratch=[pltpu.SemaphoreType.DMA((2,))],
        moved=4 * weights.size,
    )
    arrived = over_tok(blocks, 0)
    mod = lax.dynamic_slice(
        mod_table[0].transpose(1, 0, 2), (0, step[0], line * pairs * depth), (6, 1, pairs * depth)
    )[:, 0]

    states, blocks = stage(
        working(0, first_partials),
        (struct(live, depth), Leaves(count, height, 2 * group_width)),
        1,
        sizes,
        mod,
        loaded_first,
        weights,
        arrived,
        left=(3,),
        scratch=[
            pltpu.VMEM((depth, local_width), BF16),
            pltpu.SemaphoreType.DMA,
            pltpu.VMEM((count, height, 2 * group_width), BF16),
            pltpu.SemaphoreType.DMA((count,)),
        ],
    )
    blocks, weights_now = after(blocks, weights)
    arrived = over_tok(blocks, 0)
    loaded_last = stage(
        working(1, load, True, 0),
        Stays(3, depth, half_width),
        0,
        weights_now,
        left=(0,),
        scratch=[pltpu.SemaphoreType.DMA((3,))],
        moved=4 * weights.size,
    )
    leaving = lax.dynamic_slice_in_dim(weights_now, (1 - side) * half_width, half_width, 2)
    swapped_last = send(leaving, 1, 1, dt=1)
    arrived, swapped_last = after(arrived, swapped_last)

    attended, cache_first = stage(
        working(0, attention, 0),
        attended_shape,
        1,
        sizes,
        gains,
        stale,
        arrived,
        scratch=[pltpu.VMEM(kept_rows, BF16)] + attended_scratch,
    )
    arrived = over_tok(attended, 0)
    made = stage(
        working(0, layer_rows),
        struct(live, depth),
        1,
        sizes,
        mod,
        near,
        states,
        arrived,
    )
    given = send(made, 0, 1)
    across = send(made, 0, 1, df=1)
    others = send(made, 0, 1, dt=1)
    corner = send(made, 0, 1, df=1, dt=1)
    blocks = stage(
        working(1, next_partials),
        Leaves(lines, height + 16, 2 * group_width),
        1,
        sizes,
        mod,
        loaded_last,
        swapped_last,
        corner,
        others,
        across,
        given,
        scratch=[
            pltpu.VMEM((lines, height + 16, 2 * group_width), BF16),
            pltpu.SemaphoreType.DMA((lines,)),
        ],
    )
    blocks, cache_first = after(blocks, cache_first)
    arrived = over_lines(blocks, 1)
    side_first = send(cache_first, 0, 0, dt=1)
    arrived, side_first = after(arrived, side_first)

    attended, cache_last, kept_last = stage(
        working(1, attention, 1),
        attended_shape + (Stays(*kept_rows),),
        1,
        sizes,
        gains,
        stale,
        arrived,
        scratch=attended_scratch,
    )
    arrived = over_tok(attended, 1)
    side_last = send(cache_last, 1, 1, dt=1)
    arrived, side_last = after(arrived, side_last)
    blocks, pair, kept_pair = stage(
        kernel(last_rows),
        (
            Leaves(halves * count, rows, depth),
            Leaves(2, total, 2 * group_width),
            Stays(2, total, 2 * group_width),
        ),
        1,
        sizes,
        mod,
        near,
        made,
        cache_first,
        kept_last,
        side_first,
        side_last,
        given,
        across,
        arrived,
        left=(4,),
        scratch=[
            pltpu.VMEM((count, rows, depth), BF16),
            pltpu.SemaphoreType.DMA((halves,)),
            pltpu.SemaphoreType.DMA,
            pltpu.SemaphoreType.DMA,
        ],
    )
    arrived = all_devices(blocks)
    other = lax.ppermute(pair, "tok", [(t, t ^ pairs) for t in range(count)])
    final, new_cache = stage(
        kernel(join),
        (struct(1, patches, cap_dev, width), struct(2, total, local_width)),
        0,
        arrived,
        kept_pair,
        other,
        scratch=[pltpu.VMEM((groups * pairs, total, 2 * group_width), BF16)],
    )
    return final, new_cache.reshape(1, 2, patches, cap_all, local_width)


def solution(mesh):
    in_specs = (
        P(None, "tok", None),
        P(),
        P(),
        P(),
        P("section", None, None, None),
        P("section", "tok", None, "fsdp"),
        P("section", "tok", "fsdp"),
        P("section", None, None),
        P("section", None, None, None, "fsdp"),
    )
    out_specs = (P("section", None, "tok", None), P("section", None, None, None, "fsdp"))
    local = by_kernels if mesh.shape["tok"] <= MOST_PEERS else by_all_to_all
    return jax.shard_map(local, mesh=mesh, in_specs=in_specs, out_specs=out_specs, check_vma=False)
```
